256 devices in a mesh: dp: 2 (over core), dom: 128 (over y, z, x).
Axes of the slice: x: 4, y: 4, z: 8, core: 2. Of those that a mesh axis runs over, the one named last changes fastest.
Arguments:
- node_latent: bfloat16 [65536, 512], P(('dp', 'dom')), parts along dimension 0, may hold values from -6 to 6
- edge_latent: bfloat16 [524288, 512], P(('dp', 'dom')), parts along dimension 0, may hold values from -6 to 6
- edge_sender: int32 [524288], P(('dp', 'dom')), parts along dimension 0, may hold values from 0 to 767, as said below
- edge_receiver: int32 [524288], P(('dp', 'dom')), parts along dimension 0, may hold values from 0 to 255
- edge_mask: int32 [524288], P(('dp', 'dom')), parts along dimension 0, may hold values from 0 to 1, as said below
- send_list: int32 [256, 128, 4], P(('dp', 'dom')), parts along dimension 0, may hold values from -1 to 255, as said below
- edge_in: bfloat16 [2, 3, 512, 512], replicated, may hold values from -0.15625 to 0.15625
- edge_out: bfloat16 [2, 512, 512], replicated, may hold values from -0.25 to 0.25
- node_in: bfloat16 [2, 2, 512, 512], replicated, may hold values from -0.1875 to 0.1875
- node_out: bfloat16 [2, 512, 512], replicated, may hold values from -0.25 to 0.25
- biases: float32 [2, 4, 512], replicated, may hold values from -3 to 3
- ln_gain: float32 [2, 2, 512], replicated, may hold values from 0.5 to 1.5
- ln_shift: float32 [2, 2, 512], replicated, may hold values from -2 to 2
Outputs:
- node_state: bfloat16 [65536, 512], P(('dp', 'dom')), parts along dimension 0
- edge_state: bfloat16 [524288, 512], P(('dp', 'dom')), parts along dimension 0
The draws below stay inside these ranges and needn't reach their ends.
There are 2 independent parts, one for each index of `dp`. The reference program is written for one: setup_inputs(seed, part) draws one part's arguments, and reference() takes and returns one part's arrays. A program takes and returns all parts, laid end to end along the dimension named above; an argument that names none is the same for every part. Nothing has to cross between parts.
Inputs may be any that keep to these rules, and one draw needn't show every extreme that they name: send_list[p, r, k] is a local node index of partition p for k below the count of the pair (p, r) and -1 from there on; a partition sends nothing to itself, every other pair has a count of 1 to 4, and in every draw some partition receives 4 from every other one. `edge_sender`: within each partition's 2048 slots, the first half have local senders (below 256); the second half have senders 256 + p * 4 + k naming a halo slot whose send_list[p, r, k] is not -1, with r the edge's partition. `edge_mask`: within each half of a partition's slots the real edges come first; every halo slot that holds a node is the sender of some real edge.
All inputs are finite; a program needn't handle non-finite values.
Results may differ from the reference program's by a relative error of at most 0.013.
Values may be sent and summed in bfloat16 or wider, within the bound.
A program may use at most 128 MiB of HBM per device.

```python
import jax
import jax.numpy as jnp
from jax import lax

D = 512
N_DEV = 256
E_DEV = 2048
CAP = 4
ROUNDS = 2
PEERS = 128
NODES = 32768
EDGES = 262144


def partition_plan(key):
    key = jax.random.fold_in(key, 500)
    key_counts, key_full, key_remote, key_local = jax.random.split(key, 4)
    counts = jax.random.randint(key_counts, (PEERS, PEERS), 1, CAP + 1).astype(jnp.int32)
    full_target = jax.random.randint(key_full, (), 0, PEERS - 1).astype(jnp.int32)
    source = jnp.arange(PEERS, dtype=jnp.int32)[:, None]
    target = jnp.arange(PEERS, dtype=jnp.int32)[None, :]
    counts = jnp.where(target == full_target, CAP, counts)
    counts = jnp.where(source == target, 0, counts).astype(jnp.int32)
    live_total = jnp.sum(counts, axis=0).astype(jnp.int32)
    half_edges = E_DEV // 2
    remote_live = jax.random.randint(key_remote, (PEERS,), live_total, half_edges + 1).astype(jnp.int32)
    local_live = jax.random.randint(key_local, (PEERS,), half_edges // 4, half_edges + 1).astype(jnp.int32)
    return (counts, live_total, remote_live, local_live)


def draw_send_list(key, part):
    counts, live_total, remote_live, local_live = partition_plan(key)
    key = jax.random.fold_in(key, 7)
    chosen = jax.random.randint(key, (PEERS, PEERS, CAP), 0, N_DEV).astype(jnp.int32)
    item_index = jnp.arange(CAP, dtype=jnp.int32)[None, None, :]
    return jnp.where(item_index < counts[:, :, None], chosen, -1).astype(jnp.int32)


def draw_edge_sender(key, part):
    counts, live_total, remote_live, local_live = partition_plan(key)
    key = jax.random.fold_in(key, 11)
    key_pick, key_order, key_local = jax.random.split(key, 3)
    half_edges = E_DEV // 2
    item_index = jnp.arange(CAP, dtype=jnp.int32)[None, None, :]
    live_slot = (item_index < jnp.transpose(counts)[:, :, None]).reshape(PEERS, PEERS * CAP)
    live_order = jnp.argsort(1 - live_slot.astype(jnp.int32), axis=1, stable=True).astype(jnp.int32)
    position = jnp.arange(half_edges, dtype=jnp.int32)[None, :]
    picked = jax.random.randint(key_pick, (PEERS, half_edges), 0, live_total[:, None]).astype(jnp.int32)
    assigned = jnp.where(position < live_total[:, None], position, picked)
    assigned = jnp.minimum(assigned, PEERS * CAP - 1)
    slot_taken = jnp.take_along_axis(live_order, assigned, axis=1) + N_DEV
    scores = jax.random.randint(key_order, (PEERS, half_edges), 0, 2 ** 30).astype(jnp.int32)
    scores = jnp.where(position < remote_live[:, None], scores, 2 ** 30 + position)
    placed = jnp.argsort(scores, axis=1, stable=True).astype(jnp.int32)
    remote = jax.vmap(lambda where_to, values: jnp.zeros((half_edges,), jnp.int32).at[where_to].set(values))(placed, slot_taken)
    local = jax.random.randint(key_local, (PEERS, half_edges), 0, N_DEV).astype(jnp.int32)
    return jnp.concatenate([local, remote], axis=1).reshape(PEERS * E_DEV).astype(jnp.int32)


def draw_edge_mask(key, part):
    counts, live_total, remote_live, local_live = partition_plan(key)
    half_edges = E_DEV // 2
    position = jnp.arange(half_edges, dtype=jnp.int32)[None, :]
    local_mask = (position < local_live[:, None]).astype(jnp.int32)
    remote_mask = (position < remote_live[:, None]).astype(jnp.int32)
    return jnp.concatenate([local_mask, remote_mask], axis=1).reshape(PEERS * E_DEV).astype(jnp.int32)


def with_ends(array, rng, least, top_value):
    spot = [jax.random.randint(jax.random.fold_in(rng, axis), (), 0, length) for axis, length in enumerate(array.shape)]
    widest = array.shape.index(max(array.shape))
    next_to = spot[:widest] + [(spot[widest] + 1) % array.shape[widest]] + spot[widest + 1:]
    return array.at[tuple(spot)].set(least).at[tuple(next_to)].set(top_value)


def shard_levels(key, shape, pieces, least, high):
    level, own = 1.0, jax.random.fold_in(key, 6)
    for dim, parts in pieces:
        steps = jnp.exp(jax.random.uniform(jax.random.fold_in(own, dim), (parts,), jnp.float32, least / len(pieces), high / len(pieces)))
        level = level * jnp.repeat(steps, shape[dim] // parts).reshape([-1 if axis == dim else 1 for axis in range(len(shape))])
    return level


def gaussian(rng, dims, deviation, bound, shards=(), kind=jnp.bfloat16):
    values = jax.random.normal(rng, dims, jnp.float32) * deviation
    if len(shards) > 0:
        values = shard_levels(rng, dims, shards, -0.22, 0.18) * values
    return jnp.clip(values, min=-bound, max=bound).astype(kind)


def setup_inputs(seed: int = 0, part: int = 0) -> dict:
    keys = jax.random.split(jax.random.key(seed), 14)
    own_keys = jax.random.split(jax.random.fold_in(keys[13], part), 14)
    return {
        "node_latent": gaussian(own_keys[0], (NODES, D), 1.0, 6.0, ((0, 128),)),
        "edge_latent": gaussian(own_keys[1], (EDGES, D), 1.0, 6.0, ((0, 128),)),
        "edge_sender": draw_edge_sender(jax.random.fold_in(jax.random.fold_in(keys[13], part), 71), part),
        "edge_receiver": with_ends(jax.random.randint(own_keys[3], (EDGES,), 0, N_DEV), jax.random.fold_in(own_keys[3], 1), 0, N_DEV - 1).astype(jnp.int32),
        "edge_mask": draw_edge_mask(jax.random.fold_in(jax.random.fold_in(keys[13], part), 71), part),
        "send_list": draw_send_list(jax.random.fold_in(jax.random.fold_in(keys[13], part), 71), part),
        "edge_in": gaussian(keys[6], (ROUNDS, 3, D, D), (3 * D) ** -0.5, 0.15625),
        "edge_out": gaussian(keys[7], (ROUNDS, D, D), D ** -0.5, 0.25),
        "node_in": gaussian(keys[8], (ROUNDS, 2, D, D), (2 * D) ** -0.5, 0.1875),
        "node_out": gaussian(keys[9], (ROUNDS, D, D), D ** -0.5, 0.25),
        "biases": gaussian(keys[10], (ROUNDS, 4, D), 0.5, 3.0, (), jnp.float32),
        "ln_gain": jnp.clip(1.0 + 0.1 * jax.random.normal(keys[11], (ROUNDS, 2, D), jnp.float32), 0.5, 1.5),
        "ln_shift": gaussian(keys[12], (ROUNDS, 2, D), 0.3, 2.0, (), jnp.float32),
    }


def layer_norm(values, gain_vec, shift_vec):
    row_mean = lax.optimization_barrier(jnp.mean(values, axis=-1, keepdims=True))
    centered = values - row_mean
    variance = lax.optimization_barrier(jnp.mean(centered * centered, axis=-1, keepdims=True))
    return centered * lax.rsqrt(variance + 1e-05) * gain_vec + shift_vec

def reference(node_latent, edge_latent, edge_sender, edge_receiver, edge_mask, send_list, edge_in, edge_out, node_in, node_out, biases, ln_gain, ln_shift):
    edge_owner = (jnp.arange(EDGES) // E_DEV).astype(jnp.int32)
    halo_slot = jnp.maximum(edge_sender - N_DEV, 0).astype(jnp.int32)
    peer_index = (halo_slot // CAP).astype(jnp.int32)
    slot_item = (halo_slot % CAP).astype(jnp.int32)
    far_local = jnp.maximum(send_list[peer_index, edge_owner, slot_item], 0).astype(jnp.int32)
    sender_node = jnp.where(edge_sender < N_DEV, edge_owner * N_DEV + edge_sender, peer_index * N_DEV + far_local).astype(jnp.int32)
    receiver_node = (edge_owner * N_DEV + edge_receiver).astype(jnp.int32)
    live_edge = edge_mask > 0
    node_state = node_latent
    edge_state = edge_latent
    for layer_index in range(ROUNDS):
        send_proj = jnp.dot(node_state, edge_in[layer_index, 1], preferred_element_type=jnp.float32).astype(jnp.bfloat16)
        recv_proj = jnp.dot(node_state, edge_in[layer_index, 2], preferred_element_type=jnp.float32).astype(jnp.bfloat16)
        hidden = jnp.dot(edge_state, edge_in[layer_index, 0], preferred_element_type=jnp.float32)
        hidden = hidden + send_proj[sender_node].astype(jnp.float32) + recv_proj[receiver_node].astype(jnp.float32) + biases[layer_index, 0]
        activated = jax.nn.silu(hidden).astype(jnp.bfloat16)
        projected = jnp.dot(activated, edge_out[layer_index], preferred_element_type=jnp.float32) + biases[layer_index, 1]
        message = layer_norm(projected, ln_gain[layer_index, 0], ln_shift[layer_index, 0]).astype(jnp.bfloat16)
        message = jnp.where(live_edge[:, None], message, jnp.zeros((), jnp.bfloat16))
        edge_state = (edge_state.astype(jnp.float32) + message.astype(jnp.float32)).astype(jnp.bfloat16)
        aggregated = jax.ops.segment_sum(message.astype(jnp.float32), receiver_node, NODES).astype(jnp.bfloat16)
        node_hidden = jnp.dot(node_state, node_in[layer_index, 0], preferred_element_type=jnp.float32)
        node_hidden = node_hidden + jnp.dot(aggregated, node_in[layer_index, 1], preferred_element_type=jnp.float32) + biases[layer_index, 2]
        node_act = jax.nn.silu(node_hidden).astype(jnp.bfloat16)
        node_proj = jnp.dot(node_act, node_out[layer_index], preferred_element_type=jnp.float32) + biases[layer_index, 3]
        node_state = (node_state.astype(jnp.float32) + layer_norm(node_proj, ln_gain[layer_index, 1], ln_shift[layer_index, 1])).astype(jnp.bfloat16)
    return (node_state, edge_state)
```

```python
import jax
import jax.numpy as jnp
from jax import lax
from jax.experimental import pallas as pl
from jax.experimental.pallas import tpu as pltpu
from jax.sharding import PartitionSpec as P

MESH = pl.DeviceIdType.MESH
BF = jnp.bfloat16
F32 = jnp.float32

PEERS, CAP, NODES, EDGES, D = 128, 4, 256, 2048, 512
HALF = EDGES // 2
SLOTS = PEERS * CAP
NX, NZ, NY = 4, 8, 4
TILE = 256
DZ_ORDER = (4, 3, 5, 2, 6, 1, 7)


def dot(a, b):
    return jnp.dot(a, b, preferred_element_type=F32)


def silu(v):
    half = 0.5 * v
    return half * jnp.tanh(half) + half


def layer_norm(values, gain, shift):
    mean = jnp.mean(values, axis=-1, keepdims=True)
    centered = values - mean
    variance = jnp.mean(centered * centered, axis=-1, keepdims=True)
    return centered * lax.rsqrt(variance + 1e-05) * gain + shift


def swap_pairs(even, odd):
    low = lax.broadcasted_iota(jnp.int32, (1, 8, 128), 1) < 4
    first = jnp.where(low, even, pltpu.roll(odd, 4, 1))
    second = jnp.where(low, pltpu.roll(even, 4, 1), odd)
    return first, second


def kernel(
    node_hbm, edge_hbm, sender_hbm, receiver_hbm, mask_hbm, list_hbm,
    edge_in_hbm, edge_out_hbm, node_in_hbm, node_out_hbm, bias_hbm, gain_hbm, shift_hbm,
    node_out_ref, edge_out_ref,
    xl, xr, tr, agg_t, msg, hpre, wcat, w_send, w_recv, w_out, n_in, n_out,
    node_state, pick, sbuf, rbuf, halo, agg_acc, nh_pre, mask_col,
    sender_ref, receiver_ref, mask_ref, list_ref, bias_ref, gain_ref, shift_ref,
    ssem, rsem, ready, lsem, osem,
):
    me = lax.axis_index("dom")
    x, z, y = lax.rem(me, NX), lax.rem(me // NX, NZ), me // (NX * NZ)

    def peer(dx, dz, dy):
        return (lax.rem(y + dy, NY) * NZ + lax.rem(z + dz, NZ)) * NX + lax.rem(x + dx, NX)

    def tell(sem, target):
        pl.semaphore_signal(sem, inc=1, device_id={"dom": target}, device_id_type=MESH)

    barrier = pltpu.get_barrier_semaphore()
    for dz in range(1, NZ):
        tell(barrier, peer(0, dz, 0))
    for plane in range(1, NX * NY):
        tell(barrier, peer(plane % NX, 0, plane // NX))

    loads = {}

    def load(name, src, dst):
        copy = pltpu.make_async_copy(src, dst, lsem.at[len(loads)])
        copy.start()
        loads[name] = copy

    load("list", list_hbm, list_ref)
    load("node", node_hbm, node_state)
    load("send0", edge_in_hbm.at[0, 1], w_send.at[0])
    load("senders", sender_hbm, sender_ref)
    load("receivers", receiver_hbm, receiver_ref)
    load("masks", mask_hbm, mask_ref)
    load("biases", bias_hbm, bias_ref)
    load("gains", gain_hbm, gain_ref)
    load("shifts", shift_hbm, shift_ref)
    load("recv0", edge_in_hbm.at[0, 2], w_recv.at[0])
    load("edge0", edge_in_hbm.at[0, 0], wcat.at[0, pl.ds(0, D)])
    load("xl", edge_hbm.at[pl.ds(0, HALF)], xl.at[:, pl.ds(0, D)])
    load("out0", edge_out_hbm.at[0], w_out.at[0])
    load("xr", edge_hbm.at[pl.ds(HALF, HALF)], xr.at[:, pl.ds(0, D)])
    load("nin0", node_in_hbm.at[0], n_in.at[0])
    load("nout0", node_out_hbm.at[0], n_out.at[0])
    load("send1", edge_in_hbm.at[1, 1], w_send.at[1])
    load("recv1", edge_in_hbm.at[1, 2], w_recv.at[1])
    load("edge1", edge_in_hbm.at[1, 0], wcat.at[1, pl.ds(0, D)])
    load("out1", edge_out_hbm.at[1], w_out.at[1])
    load("nin1", node_in_hbm.at[1], n_in.at[1])
    load("nout1", node_out_hbm.at[1], n_out.at[1])

    slot_row = lax.broadcasted_iota(jnp.int32, (SLOTS, PEERS), 0)
    spread = (slot_row // CAP == lax.broadcasted_iota(jnp.int32, (SLOTS, PEERS), 1)).astype(BF)
    loads["list"].wait()
    lists = lax.dot_general(
        spread, list_ref[...].astype(F32).astype(BF), (((1,), (1,)), ((), ())), preferred_element_type=F32
    )
    own = lax.broadcasted_iota(jnp.int32, (SLOTS, CAP), 0) % CAP == lax.broadcasted_iota(
        jnp.int32, (SLOTS, CAP), 1
    )
    chosen = jnp.sum(jnp.where(own, lists, 0.0), axis=1, keepdims=True).astype(jnp.int32)
    pick[...] = (chosen == lax.broadcasted_iota(jnp.int32, (SLOTS, NODES), 1)).astype(BF)
    for r in range(2):
        rbuf[r, me] = jnp.zeros((16, 128), BF)

    def project_and_pack(r):
        loads[f"send{r}"].wait()
        send_proj = dot(node_state[...], w_send[r]).astype(BF)
        wcat[r, pl.ds(D + NODES, NODES), :] = send_proj
        rows = dot(pick[...], send_proj)
        for h in range(2):
            first, second = swap_pairs(
                rows[:, 256 * h : 256 * h + 128].reshape(PEERS // 2, 8, 128),
                rows[:, 256 * h + 128 : 256 * h + 256].reshape(PEERS // 2, 8, 128),
            )
            part = jnp.stack([first, second], axis=1).reshape(PEERS, 8, 128)
            if h == 0:
                upper = part
        sbuf[...] = jnp.concatenate([upper, part], axis=1).astype(BF)

    def send(r, target):
        pltpu.make_async_remote_copy(
            src_ref=sbuf.at[target],
            dst_ref=rbuf.at[r, me],
            send_sem=ssem.at[r],
            recv_sem=rsem.at[r],
            device_id={"dom": target},
            device_id_type=MESH,
        ).start()

    def send_far(r):
        def body(j, carry):
            plane = NX * NY - 1 - j
            for dz in DZ_ORDER:
                send(r, peer(lax.rem(plane, NX), dz, plane // NX))
            return carry

        lax.fori_loop(0, NX * NY - 1, body, 0)

    def send_line(r):
        for dz in DZ_ORDER:
            send(r, peer(0, dz, 0))

    def send_plane(r):
        def body(plane, carry):
            send(r, peer(lax.rem(plane, NX), 0, plane // NX))
            return carry

        lax.fori_loop(1, NX * NY, body, 0)

    def receive(r):
        everything = pltpu.make_async_remote_copy(
            src_ref=sbuf.at[pl.ds(0, PEERS - 1)],
            dst_ref=rbuf.at[r, pl.ds(0, PEERS - 1)],
            send_sem=ssem.at[r],
            recv_sem=rsem.at[r],
            device_id={"dom": lax.rem(me + 1, PEERS)},
            device_id_type=MESH,
        )
        everything.wait_send()
        everything.wait_recv()
        got = rbuf[r].astype(F32).reshape(PEERS // 2, 2, 2, 8, 128)
        for h in range(2):
            first, second = swap_pairs(got[:, 0, h], got[:, 1, h])
            halo[:, 256 * h : 256 * h + 128] = first.reshape(SLOTS, 128).astype(BF)
            halo[:, 256 * h + 128 : 256 * h + 256] = second.reshape(SLOTS, 128).astype(BF)

    def tables():
        senders = jnp.transpose(sender_ref[...])
        receivers = jnp.transpose(receiver_ref[...])
        masks = jnp.transpose(mask_ref[...])
        nodes = lax.broadcasted_iota(jnp.int32, (128, NODES), 1)
        slots = lax.broadcasted_iota(jnp.int32, (128, SLOTS), 1)
        node_rows = lax.broadcasted_iota(jnp.int32, (NODES, 128), 0)
        for j in range(EDGES // 128):
            rows = pl.ds(j % 8 * 128, 128)
            mask_col[pl.ds(j * 128, 128), :] = masks[:, j : j + 1].astype(F32)
            received = (receivers[:, j : j + 1] == nodes).astype(BF)
            if j < 8:
                xl[rows, pl.ds(D, NODES)] = received
                xl[rows, pl.ds(D + NODES, NODES)] = (senders[:, j : j + 1] == nodes).astype(BF)
            else:
                xr[rows, pl.ds(D, NODES)] = received
                tr[rows, :] = (senders[:, j : j + 1] - NODES == slots).astype(BF)
            live = jnp.where(mask_ref[j : j + 1, :] > 0, receiver_ref[j : j + 1, :], -1)
            agg_t[:, pl.ds(j * 128, 128)] = (live == node_rows).astype(BF)

    def edge_tail(r, hidden, state, live):
        act = silu(hidden).astype(BF)
        projected = dot(act, w_out[r]) + bias_ref[r, 1:2, :]
        message = layer_norm(projected, gain_ref[r, 0:1, :], shift_ref[r, 0:1, :]).astype(BF)
        kept = jnp.where(live > 0, message.astype(F32), 0.0)
        return message, (state.astype(F32) + kept).astype(BF)

    def local_edges(r):
        def body(t, carry):
            rows = pl.ds(pl.multiple_of(t * TILE, TILE), TILE)
            hidden = dot(xl[rows, :], wcat[r]) + bias_ref[r, 0:1, :]
            message, state = edge_tail(r, hidden, xl[rows, pl.ds(0, D)], mask_col[rows, :])
            xl[rows, pl.ds(0, D)] = state
            msg[rows, :] = message
            return carry

        lax.fori_loop(0, HALF // TILE, body, 0)
        agg_acc[...] = dot(agg_t[:, pl.ds(0, HALF)], msg[...])

    def remote_start(r):
        def body(t, carry):
            rows = pl.ds(pl.multiple_of(t * TILE, TILE), TILE)
            hpre[rows, :] = dot(xr[rows, :], wcat[r, pl.ds(0, D + NODES), :]) + bias_ref[r, 0:1, :]
            return carry

        lax.fori_loop(0, HALF // TILE, body, 0)

    def remote_edges(r):
        def body(t, carry):
            rows = pl.ds(pl.multiple_of(t * TILE, TILE), TILE)
            masks = mask_col[pl.ds(pl.multiple_of(HALF + t * TILE, TILE), TILE), :]
            hidden = dot(tr[rows, :], halo[...]) + hpre[rows, :]
            message, state = edge_tail(r, hidden, xr[rows, pl.ds(0, D)], masks)
            xr[rows, pl.ds(0, D)] = state
            msg[rows, :] = message
            return carry

        lax.fori_loop(0, HALF // TILE, body, 0)

    def write(k, src, dst):
        copy = pltpu.make_async_copy(src, dst, osem.at[k])
        copy.start()
        return copy

    loads["node"].wait()
    project_and_pack(0)
    pl.semaphore_wait(barrier, NZ - 1 + NX * NY - 1)
    for plane in range(1, NX * NY):
        tell(ready, peer(plane % NX, 0, plane // NX))
    send_line(0)
    pl.semaphore_wait(ready, NX * NY - 1)
    send_far(0)
    send_plane(0)
    for name in ("senders", "receivers", "masks", "biases", "gains", "shifts"):
        loads[name].wait()
    tables()

    writes = []
    for r in range(2):
        loads[f"recv{r}"].wait()
        wcat[r, pl.ds(D, NODES), :] = dot(node_state[...], w_recv[r]).astype(BF)
        if r == 0:
            loads["xl"].wait()
            loads["xr"].wait()
        loads[f"edge{r}"].wait()
        loads[f"out{r}"].wait()
        local_edges(r)
        if r == 1:
            writes.append(write(0, xl.at[:, pl.ds(0, D)], edge_out_ref.at[pl.ds(0, HALF)]))
        remote_start(r)
        loads[f"nin{r}"].wait()
        loads[f"nout{r}"].wait()
        nh_pre[...] = dot(node_state[...], n_in[r, 0]) + bias_ref[r, 2:3, :]
        receive(r)
        remote_edges(r)
        if r == 1:
            writes.append(write(1, xr.at[:, pl.ds(0, D)], edge_out_ref.at[pl.ds(HALF, HALF)]))
        total = (agg_acc[...] + dot(agg_t[:, pl.ds(HALF, HALF)], msg[...])).astype(BF)
        act = silu(nh_pre[...] + dot(total, n_in[r, 1])).astype(BF)
        projected = dot(act, n_out[r]) + bias_ref[r, 3:4, :]
        update = layer_norm(projected, gain_ref[r, 1:2, :], shift_ref[r, 1:2, :])
        node_state[...] = (node_state[...].astype(F32) + update).astype(BF)
        if r == 0:
            project_and_pack(1)
            send_far(1)
            send_line(1)
            send_plane(1)
    writes.append(write(2, node_state, node_out_ref))
    for copy in writes:
        copy.wait()


def local(
    node_latent, edge_latent, edge_sender, edge_receiver, edge_mask, send_list,
    edge_in, edge_out, node_in, node_out, biases, ln_gain, ln_shift,
):
    hbm = pl.BlockSpec(memory_space=pltpu.HBM)
    return pl.pallas_call(
        kernel,
        out_shape=(
            jax.ShapeDtypeStruct((NODES, D), BF),
            jax.ShapeDtypeStruct((EDGES, D), BF),
        ),
        in_specs=[hbm] * 13,
        out_specs=(hbm, hbm),
        scratch_shapes=[
            pltpu.VMEM((HALF, D + 2 * NODES), BF),
            pltpu.VMEM((HALF, D + NODES), BF),
            pltpu.VMEM((HALF, SLOTS), BF),
            pltpu.VMEM((NODES, EDGES), BF),
            pltpu.VMEM((HALF, D), BF),
            pltpu.VMEM((HALF, D), F32),
            pltpu.VMEM((2, D + 2 * NODES, D), BF),
            pltpu.VMEM((2, D, D), BF),
            pltpu.VMEM((2, D, D), BF),
            pltpu.VMEM((2, D, D), BF),
            pltpu.VMEM((2, 2, D, D), BF),
            pltpu.VMEM((2, D, D), BF),
            pltpu.VMEM((NODES, D), BF),
            pltpu.VMEM((SLOTS, NODES), BF),
            pltpu.VMEM((PEERS, 16, 128), BF),
            pltpu.VMEM((2, PEERS, 16, 128), BF),
            pltpu.VMEM((SLOTS, D), BF),
            pltpu.VMEM((NODES, D), F32),
            pltpu.VMEM((NODES, D), F32),
            pltpu.VMEM((EDGES, 1), F32),
            pltpu.VMEM((16, 128), jnp.int32),
            pltpu.VMEM((16, 128), jnp.int32),
            pltpu.VMEM((16, 128), jnp.int32),
            pltpu.VMEM((CAP, PEERS), jnp.int32),
            pltpu.VMEM((2, 4, D), F32),
            pltpu.VMEM((2, 2, D), F32),
            pltpu.VMEM((2, 2, D), F32),
            pltpu.SemaphoreType.DMA((2,)),
            pltpu.SemaphoreType.DMA((2,)),
            pltpu.SemaphoreType.REGULAR,
            pltpu.SemaphoreType.DMA((22,)),
            pltpu.SemaphoreType.DMA((3,)),
        ],
        compiler_params=pltpu.CompilerParams(
            collective_id=0, has_side_effects=True, vmem_limit_bytes=52 * 2**20
        ),
    )(
        node_latent, edge_latent,
        edge_sender.reshape(16, 128), edge_receiver.reshape(16, 128), edge_mask.reshape(16, 128),
        send_list.reshape(PEERS, CAP).T,
        edge_in, edge_out, node_in, node_out, biases, ln_gain, ln_shift,
    )


def solution(mesh):
    in_specs = (
        P(("dp", "dom"), None),
        P(("dp", "dom"), None),
        P(("dp", "dom")),
        P(("dp", "dom")),
        P(("dp", "dom")),
        P(("dp", "dom"), None, None),
        P(),
        P(),
        P(),
        P(),
        P(),
        P(),
        P(),
    )
    out_specs = (P(("dp", "dom"), None), P(("dp", "dom"), None))
    return jax.shard_map(local, mesh=mesh, in_specs=in_specs, out_specs=out_specs, check_vma=False)
```

```python
import jax
import jax.numpy as jnp
from jax import lax
from jax.experimental import pallas as pl
from jax.experimental.pallas import tpu as pltpu
from jax.sharding import PartitionSpec as P

MESH = pl.DeviceIdType.MESH
BF = jnp.bfloat16
F32 = jnp.float32

PEERS, CAP, NODES, EDGES, D = 128, 4, 256, 2048, 512
HALF = EDGES // 2
SLOTS = PEERS * CAP
NX, NZ, NY = 4, 8, 4
TILE = 256
DZ_ORDER = (4, 3, 5, 2, 6, 1, 7)


def dot(a, b):
    return jnp.dot(a, b, preferred_element_type=F32)


def silu(v):
    half = 0.5 * v
    return half * jnp.tanh(half) + half


def layer_norm(values, gain, shift):
    mean = jnp.mean(values, axis=-1, keepdims=True)
    centered = values - mean
    variance = jnp.mean(centered * centered, axis=-1, keepdims=True)
    return centered * lax.rsqrt(variance + 1e-05) * gain + shift


def swap_pairs(even, odd):
    low = lax.broadcasted_iota(jnp.int32, (1, 8, 128), 1) < 4
    first = jnp.where(low, even, pltpu.roll(odd, 4, 1))
    second = jnp.where(low, pltpu.roll(even, 4, 1), odd)
    return first, second


def edge_tail(hidden, state, live, w_out, bias, gain, shift):
    act = silu(hidden).astype(BF)
    projected = dot(act, w_out) + bias[1:2, :]
    message = layer_norm(projected, gain[0:1, :], shift[0:1, :]).astype(BF)
    kept = jnp.where(live > 0, message.astype(F32), 0.0)
    return message, (state.astype(F32) + kept).astype(BF)


def remote_edges(tr, halo, hpre, xr, mask_col, msg, state_ref, w_out, bias, gain, shift):
    def body(t, carry):
        rows = pl.ds(pl.multiple_of(t * TILE, TILE), TILE)
        masks = mask_col[pl.ds(pl.multiple_of(HALF + t * TILE, TILE), TILE), :]
        hidden = dot(tr[rows, :], halo[...]) + hpre[rows, :]
        message, state = edge_tail(hidden, xr[rows, pl.ds(0, D)], masks, w_out, bias, gain, shift)
        state_ref[rows, pl.ds(0, D)] = state
        msg[rows, :] = message
        return carry

    lax.fori_loop(0, HALF // TILE, body, 0)


def node_step(agg_acc, agg_t, msg, nh_pre, node_state, w_in, w_out, bias, gain, shift):
    total = (agg_acc[...] + dot(agg_t[:, pl.ds(HALF, HALF)], msg[...])).astype(BF)
    act = silu(nh_pre[...] + dot(total, w_in)).astype(BF)
    projected = dot(act, w_out) + bias[3:4, :]
    update = layer_norm(projected, gain[1:2, :], shift[1:2, :])
    return (node_state[...].astype(F32) + update).astype(BF)


def kernel(
    node_hbm, edge_hbm, sender_hbm, receiver_hbm, mask_hbm, list_hbm,
    edge_in_hbm, edge_out_hbm, node_in_hbm, node_out_hbm, bias_hbm, gain_hbm, shift_hbm,
    xl, xr, tr, agg_t, hpre, halo, agg_acc, nh_pre, node_state, mask_col,
    w_out, n_in, n_out, bias_ref, gain_ref, shift_ref,
    msg, wcat, w_send, w_recv, pick, sbuf, rbuf,
    sender_ref, receiver_ref, mask_ref, list_ref,
    ssem, rsem, ready, lsem,
):
    me = lax.axis_index("dom")
    x, z, y = lax.rem(me, NX), lax.rem(me // NX, NZ), me // (NX * NZ)

    def peer(dx, dz, dy):
        return (lax.rem(y + dy, NY) * NZ + lax.rem(z + dz, NZ)) * NX + lax.rem(x + dx, NX)

    def tell(sem, target):
        pl.semaphore_signal(sem, inc=1, device_id={"dom": target}, device_id_type=MESH)

    barrier = pltpu.get_barrier_semaphore()
    for dz in range(1, NZ):
        tell(barrier, peer(0, dz, 0))
    for plane in range(1, NX * NY):
        tell(barrier, peer(plane % NX, 0, plane // NX))

    loads = {}

    def load(name, src, dst):
        copy = pltpu.make_async_copy(src, dst, lsem.at[len(loads)])
        copy.start()
        loads[name] = copy

    load("list", list_hbm, list_ref)
    load("node", node_hbm, node_state)
    load("send0", edge_in_hbm.at[0, 1], w_send.at[0])
    load("senders", sender_hbm, sender_ref)
    load("receivers", receiver_hbm, receiver_ref)
    load("masks", mask_hbm, mask_ref)
    load("biases", bias_hbm, bias_ref)
    load("gains", gain_hbm, gain_ref)
    load("shifts", shift_hbm, shift_ref)
    load("recv0", edge_in_hbm.at[0, 2], w_recv.at[0])
    load("edge0", edge_in_hbm.at[0, 0], wcat.at[0, pl.ds(0, D)])
    load("xl", edge_hbm.at[pl.ds(0, HALF)], xl.at[:, pl.ds(0, D)])
    load("out0", edge_out_hbm.at[0], w_out.at[0])
    load("xr", edge_hbm.at[pl.ds(HALF, HALF)], xr.at[:, pl.ds(0, D)])
    load("nin0", node_in_hbm.at[0], n_in.at[0])
    load("nout0", node_out_hbm.at[0], n_out.at[0])
    load("send1", edge_in_hbm.at[1, 1], w_send.at[1])
    load("recv1", edge_in_hbm.at[1, 2], w_recv.at[1])
    load("edge1", edge_in_hbm.at[1, 0], wcat.at[1, pl.ds(0, D)])
    load("out1", edge_out_hbm.at[1], w_out.at[1])
    load("nin1", node_in_hbm.at[1], n_in.at[1])
    load("nout1", node_out_hbm.at[1], n_out.at[1])

    slot_row = lax.broadcasted_iota(jnp.int32, (SLOTS, PEERS), 0)
    spread = (slot_row // CAP == lax.broadcasted_iota(jnp.int32, (SLOTS, PEERS), 1)).astype(BF)
    loads["list"].wait()
    lists = lax.dot_general(
        spread, list_ref[...].astype(F32).astype(BF), (((1,), (1,)), ((), ())), preferred_element_type=F32
    )
    own = lax.broadcasted_iota(jnp.int32, (SLOTS, CAP), 0) % CAP == lax.broadcasted_iota(
        jnp.int32, (SLOTS, CAP), 1
    )
    chosen = jnp.sum(jnp.where(own, lists, 0.0), axis=1, keepdims=True).astype(jnp.int32)
    pick[...] = (chosen == lax.broadcasted_iota(jnp.int32, (SLOTS, NODES), 1)).astype(BF)
    for r in range(2):
        rbuf[r, me] = jnp.zeros((16, 128), BF)

    def project_and_pack(r):
        loads[f"send{r}"].wait()
        send_proj = dot(node_state[...], w_send[r]).astype(BF)
        wcat[r, pl.ds(D + NODES, NODES), :] = send_proj
        rows = dot(pick[...], send_proj)
        for h in range(2):
            first, second = swap_pairs(
                rows[:, 256 * h : 256 * h + 128].reshape(PEERS // 2, 8, 128),
                rows[:, 256 * h + 128 : 256 * h + 256].reshape(PEERS // 2, 8, 128),
            )
            part = jnp.stack([first, second], axis=1).reshape(PEERS, 8, 128)
            if h == 0:
                upper = part
        sbuf[...] = jnp.concatenate([upper, part], axis=1).astype(BF)

    def send(r, target):
        pltpu.make_async_remote_copy(
            src_ref=sbuf.at[target],
            dst_ref=rbuf.at[r, me],
            send_sem=ssem.at[r],
            recv_sem=rsem.at[r],
            device_id={"dom": target},
            device_id_type=MESH,
        ).start()

    def send_far(r):
        def body(j, carry):
            plane = NX * NY - 1 - j
            for dz in DZ_ORDER:
                send(r, peer(lax.rem(plane, NX), dz, plane // NX))
            return carry

        lax.fori_loop(0, NX * NY - 1, body, 0)

    def send_line(r):
        for dz in DZ_ORDER:
            send(r, peer(0, dz, 0))

    def send_plane(r):
        def body(plane, carry):
            send(r, peer(lax.rem(plane, NX), 0, plane // NX))
            return carry

        lax.fori_loop(1, NX * NY, body, 0)

    def receive(r):
        everything = pltpu.make_async_remote_copy(
            src_ref=sbuf.at[pl.ds(0, PEERS - 1)],
            dst_ref=rbuf.at[r, pl.ds(0, PEERS - 1)],
            send_sem=ssem.at[r],
            recv_sem=rsem.at[r],
            device_id={"dom": lax.rem(me + 1, PEERS)},
            device_id_type=MESH,
        )
        everything.wait_send()
        everything.wait_recv()
        got = rbuf[r].astype(F32).reshape(PEERS // 2, 2, 2, 8, 128)
        for h in range(2):
            first, second = swap_pairs(got[:, 0, h], got[:, 1, h])
            halo[:, 256 * h : 256 * h + 128] = first.reshape(SLOTS, 128).astype(BF)
            halo[:, 256 * h + 128 : 256 * h + 256] = second.reshape(SLOTS, 128).astype(BF)

    def tables():
        senders = jnp.transpose(sender_ref[...])
        receivers = jnp.transpose(receiver_ref[...])
        masks = jnp.transpose(mask_ref[...])
        nodes = lax.broadcasted_iota(jnp.int32, (128, NODES), 1)
        slots = lax.broadcasted_iota(jnp.int32, (128, SLOTS), 1)
        node_rows = lax.broadcasted_iota(jnp.int32, (NODES, 128), 0)
        for j in range(EDGES // 128):
            rows = pl.ds(j % 8 * 128, 128)
            mask_col[pl.ds(j * 128, 128), :] = masks[:, j : j + 1].astype(F32)
            received = (receivers[:, j : j + 1] == nodes).astype(BF)
            if j < 8:
                xl[rows, pl.ds(D, NODES)] = received
                xl[rows, pl.ds(D + NODES, NODES)] = (senders[:, j : j + 1] == nodes).astype(BF)
            else:
                xr[rows, pl.ds(D, NODES)] = received
                tr[rows, :] = (senders[:, j : j + 1] - NODES == slots).astype(BF)
            live = jnp.where(mask_ref[j : j + 1, :] > 0, receiver_ref[j : j + 1, :], -1)
            agg_t[:, pl.ds(j * 128, 128)] = (live == node_rows).astype(BF)

    def local_edges(r):
        def body(t, carry):
            rows = pl.ds(pl.multiple_of(t * TILE, TILE), TILE)
            hidden = dot(xl[rows, :], wcat[r]) + bias_ref[r, 0:1, :]
            message, state = edge_tail(
                hidden, xl[rows, pl.ds(0, D)], mask_col[rows, :],
                w_out[r], bias_ref[r], gain_ref[r], shift_ref[r],
            )
            xl[rows, pl.ds(0, D)] = state
            msg[rows, :] = message
            return carry

        lax.fori_loop(0, HALF // TILE, body, 0)
        agg_acc[...] = dot(agg_t[:, pl.ds(0, HALF)], msg[...])

    def remote_start(r):
        def body(t, carry):
            rows = pl.ds(pl.multiple_of(t * TILE, TILE), TILE)
            hpre[rows, :] = dot(xr[rows, :], wcat[r, pl.ds(0, D + NODES), :]) + bias_ref[r, 0:1, :]
            return carry

        lax.fori_loop(0, HALF // TILE, body, 0)

    loads["node"].wait()
    project_and_pack(0)
    pl.semaphore_wait(barrier, NZ - 1 + NX * NY - 1)
    for plane in range(1, NX * NY):
        tell(ready, peer(plane % NX, 0, plane // NX))
    send_line(0)
    pl.semaphore_wait(ready, NX * NY - 1)
    send_far(0)
    send_plane(0)
    for name in ("senders", "receivers", "masks", "biases", "gains", "shifts"):
        loads[name].wait()
    tables()

    for r in range(2):
        loads[f"recv{r}"].wait()
        wcat[r, pl.ds(D, NODES), :] = dot(node_state[...], w_recv[r]).astype(BF)
        if r == 0:
            loads["xl"].wait()
            loads["xr"].wait()
        loads[f"edge{r}"].wait()
        loads[f"out{r}"].wait()
        local_edges(r)
        remote_start(r)
        loads[f"nin{r}"].wait()
        loads[f"nout{r}"].wait()
        nh_pre[...] = dot(node_state[...], n_in[r, 0]) + bias_ref[r, 2:3, :]
        receive(r)
        if r == 0:
            remote_edges(
                tr, halo, hpre, xr, mask_col, msg, xr,
                w_out[r], bias_ref[r], gain_ref[r], shift_ref[r],
            )
            node_state[...] = node_step(
                agg_acc, agg_t, msg, nh_pre, node_state,
                n_in[r, 1], n_out[r], bias_ref[r], gain_ref[r], shift_ref[r],
            )
            project_and_pack(1)
            send_far(1)
            send_line(1)
            send_plane(1)


def finish(
    xl, xr, tr, agg_t, hpre, halo, agg_acc, nh_pre, node_state, mask_col,
    w_out, n_in, n_out, bias_ref, gain_ref, shift_ref,
    node_out_hbm, edge_out_hbm,
    msg, state, node_new, osem,
):
    near = pltpu.make_async_copy(xl.at[:, pl.ds(0, D)], edge_out_hbm.at[pl.ds(0, HALF)], osem.at[0])
    near.start()
    remote_edges(
        tr, halo, hpre, xr, mask_col, msg, state,
        w_out[1], bias_ref[1], gain_ref[1], shift_ref[1],
    )
    far = pltpu.make_async_copy(state, edge_out_hbm.at[pl.ds(HALF, HALF)], osem.at[1])
    far.start()
    node_new[...] = node_step(
        agg_acc, agg_t, msg, nh_pre, node_state,
        n_in[1, 1], n_out[1], bias_ref[1], gain_ref[1], shift_ref[1],
    )
    nodes = pltpu.make_async_copy(node_new, node_out_hbm, osem.at[2])
    nodes.start()
    near.wait()
    far.wait()
    nodes.wait()


def local(
    node_latent, edge_latent, edge_sender, edge_receiver, edge_mask, send_list,
    edge_in, edge_out, node_in, node_out, biases, ln_gain, ln_shift,
):
    hbm = pl.BlockSpec(memory_space=pltpu.HBM)
    vmem = pl.BlockSpec(memory_space=pltpu.VMEM)
    args = [
        node_latent, edge_latent,
        edge_sender.reshape(16, 128), edge_receiver.reshape(16, 128), edge_mask.reshape(16, 128),
        send_list.reshape(PEERS, CAP).T,
        edge_in, edge_out, node_in, node_out, biases, ln_gain, ln_shift,
    ]
    held = (
        pltpu.VMEM((HALF, D + 2 * NODES), BF),
        pltpu.VMEM((HALF, D + NODES), BF),
        pltpu.VMEM((HALF, SLOTS), BF),
        pltpu.VMEM((NODES, EDGES), BF),
        pltpu.VMEM((HALF, D), F32),
        pltpu.VMEM((SLOTS, D), BF),
        pltpu.VMEM((NODES, D), F32),
        pltpu.VMEM((NODES, D), F32),
        pltpu.VMEM((NODES, D), BF),
        pltpu.VMEM((EDGES, 1), F32),
        pltpu.VMEM((2, D, D), BF),
        pltpu.VMEM((2, 2, D, D), BF),
        pltpu.VMEM((2, D, D), BF),
        pltpu.VMEM((2, 4, D), F32),
        pltpu.VMEM((2, 2, D), F32),
        pltpu.VMEM((2, 2, D), F32),
    )
    passed = pl.pallas_call(
        kernel,
        out_shape=held,
        in_specs=[hbm] * 13,
        out_specs=(vmem,) * len(held),
        scratch_shapes=[
            pltpu.VMEM((HALF, D), BF),
            pltpu.VMEM((2, D + 2 * NODES, D), BF),
            pltpu.VMEM((2, D, D), BF),
            pltpu.VMEM((2, D, D), BF),
            pltpu.VMEM((SLOTS, NODES), BF),
            pltpu.VMEM((PEERS, 16, 128), BF),
            pltpu.VMEM((2, PEERS, 16, 128), BF),
            pltpu.VMEM((16, 128), jnp.int32),
            pltpu.VMEM((16, 128), jnp.int32),
            pltpu.VMEM((16, 128), jnp.int32),
            pltpu.VMEM((CAP, PEERS), jnp.int32),
            pltpu.SemaphoreType.DMA((2,)),
            pltpu.SemaphoreType.DMA((2,)),
            pltpu.SemaphoreType.REGULAR,
            pltpu.SemaphoreType.DMA((22,)),
        ],
        compiler_params=pltpu.CompilerParams(
            collective_id=0, has_side_effects=True, vmem_limit_bytes=28 * 2**20
        ),
    )(*[pltpu.with_memory_space_constraint(a, pltpu.HBM) for a in args])
    return pl.pallas_call(
        finish,
        out_shape=(pltpu.HBM((NODES, D), BF), pltpu.HBM((EDGES, D), BF)),
        in_specs=[vmem] * len(held),
        out_specs=(hbm, hbm),
        scratch_shapes=[
            pltpu.VMEM((HALF, D), BF),
            pltpu.VMEM((HALF, D), BF),
            pltpu.VMEM((NODES, D), BF),
            pltpu.SemaphoreType.DMA((3,)),
        ],
        compiler_params=pltpu.CompilerParams(vmem_limit_bytes=20 * 2**20),
    )(*passed)


def solution(mesh):
    in_specs = (
        P(("dp", "dom"), None),
        P(("dp", "dom"), None),
        P(("dp", "dom")),
        P(("dp", "dom")),
        P(("dp", "dom")),
        P(("dp", "dom"), None, None),
        P(),
        P(),
        P(),
        P(),
        P(),
        P(),
        P(),
    )
    out_specs = (P(("dp", "dom"), None), P(("dp", "dom"), None))
    return jax.shard_map(local, mesh=mesh, in_specs=in_specs, out_specs=out_specs, check_vma=False)
```

```python
import jax
import jax.numpy as jnp
from jax import lax
from jax.experimental import pallas as pl
from jax.experimental.pallas import tpu as pltpu
from jax.sharding import PartitionSpec as P

MESH = pl.DeviceIdType.MESH
BF = jnp.bfloat16
F32 = jnp.float32

PEERS, CAP, NODES, EDGES, D = 128, 4, 256, 2048, 512
HALF = EDGES // 2
SLOTS = PEERS * CAP
NX, NZ, NY = 4, 8, 4
TILE = 512
DZ_ORDER = (4, 3, 5, 2, 6, 1, 7)


def dot(a, b):
    return jnp.dot(a, b, preferred_element_type=F32)


def silu(v):
    half = 0.5 * v
    return half * jnp.tanh(half) + half


def layer_norm(values, gain, shift):
    mean = jnp.mean(values, axis=-1, keepdims=True)
    centered = values - mean
    variance = jnp.mean(centered * centered, axis=-1, keepdims=True)
    return centered * lax.rsqrt(variance + 1e-05) * gain + shift


def swap_pairs(even, odd):
    low = lax.broadcasted_iota(jnp.int32, (1, 8, 128), 1) < 4
    first = jnp.where(low, even, pltpu.roll(odd, 4, 1))
    second = jnp.where(low, pltpu.roll(even, 4, 1), odd)
    return first, second


def edge_tail(hidden, state, live, w_out, bias, gain, shift):
    act = silu(hidden).astype(BF)
    projected = dot(act, w_out) + bias[1:2, :]
    message = layer_norm(projected, gain[0:1, :], shift[0:1, :])
    message = jnp.where(live > 0, message, 0.0).astype(BF)
    return message, state + message


def remote_edges(tr, halo, hpre, xr, mask_col, msg, state_ref, w_out, bias, gain, shift):
    def body(t, carry):
        rows = pl.ds(pl.multiple_of(t * TILE, TILE), TILE)
        masks = mask_col[pl.ds(pl.multiple_of(HALF + t * TILE, TILE), TILE), :]
        hidden = dot(tr[rows, :], halo[...]) + hpre[rows, :]
        message, state = edge_tail(hidden, xr[rows, pl.ds(0, D)], masks, w_out, bias, gain, shift)
        state_ref[rows, pl.ds(0, D)] = state
        msg[rows, :] = message
        return carry

    lax.fori_loop(0, HALF // TILE, body, 0, unroll=True)


def node_step(agg_acc, agg_t, msg, nh_pre, node_state, w_in, w_out, bias, gain, shift):
    total = (agg_acc[...] + dot(agg_t[:, pl.ds(HALF, HALF)], msg[...])).astype(BF)
    act = silu(nh_pre[...] + dot(total, w_in)).astype(BF)
    projected = dot(act, w_out) + bias[3:4, :]
    update = layer_norm(projected, gain[1:2, :], shift[1:2, :])
    return (node_state[...].astype(F32) + update).astype(BF)


def kernel(
    node_hbm, edge_hbm, sender_hbm, receiver_hbm, mask_hbm, list_hbm,
    edge_in_hbm, edge_out_hbm, node_in_hbm, node_out_hbm, bias_hbm, gain_hbm, shift_hbm,
    xl, xr, tr, agg_t, hpre, halo, agg_acc, nh_pre, node_state, mask_col,
    w_out, n_in, n_out, bias_ref, gain_ref, shift_ref,
    msg, wcat, w_send, w_recv, pick, sbuf, rbuf,
    sender_ref, receiver_ref, mask_ref, list_ref,
    ssem, rsem, ready, lsem,
):
    me = lax.axis_index("dom")
    x, z, y = lax.rem(me, NX), lax.rem(me // NX, NZ), me // (NX * NZ)

    def peer(dx, dz, dy):
        return (lax.rem(y + dy, NY) * NZ + lax.rem(z + dz, NZ)) * NX + lax.rem(x + dx, NX)

    def tell(sem, target):
        pl.semaphore_signal(sem, inc=1, device_id={"dom": target}, device_id_type=MESH)

    loads = {}

    def load(name, src, dst):
        copy = pltpu.make_async_copy(src, dst, lsem.at[len(loads)])
        copy.start()
        loads[name] = copy

    load("list", list_hbm, list_ref)
    load("node", node_hbm, node_state)
    load("send0", edge_in_hbm.at[0, 1], w_send.at[0])

    barrier = pltpu.get_barrier_semaphore()
    for plane in range(1, NX * NY):
        tell(barrier, peer(plane % NX, 0, plane // NX))
    for dz in range(1, NZ):
        tell(barrier, peer(0, dz, 0))

    slot_row = lax.broadcasted_iota(jnp.int32, (SLOTS, PEERS), 0)
    spread = (slot_row // CAP == lax.broadcasted_iota(jnp.int32, (SLOTS, PEERS), 1)).astype(BF)
    loads["list"].wait()
    lists = lax.dot_general(
        spread, list_ref[...].astype(F32).astype(BF), (((1,), (1,)), ((), ())), preferred_element_type=F32
    )
    own = lax.broadcasted_iota(jnp.int32, (SLOTS, CAP), 0) % CAP == lax.broadcasted_iota(
        jnp.int32, (SLOTS, CAP), 1
    )
    chosen = jnp.sum(jnp.where(own, lists, 0.0), axis=1, keepdims=True).astype(jnp.int32)
    pick[...] = (chosen == lax.broadcasted_iota(jnp.int32, (SLOTS, NODES), 1)).astype(BF)
    for r in range(2):
        rbuf[r, me] = jnp.zeros((16, 128), BF)

    def project_and_pack(r):
        loads[f"send{r}"].wait()
        send_proj = dot(node_state[...], w_send[r]).astype(BF)
        wcat[r, pl.ds(D + NODES, NODES), :] = send_proj
        rows = dot(pick[...], send_proj)
        for h in range(2):
            first, second = swap_pairs(
                rows[:, 256 * h : 256 * h + 128].reshape(PEERS // 2, 8, 128),
                rows[:, 256 * h + 128 : 256 * h + 256].reshape(PEERS // 2, 8, 128),
            )
            part = jnp.stack([first, second], axis=1).reshape(PEERS, 8, 128)
            if h == 0:
                upper = part
        sbuf[...] = jnp.concatenate([upper, part], axis=1).astype(BF)

    def send(r, target):
        pltpu.make_async_remote_copy(
            src_ref=sbuf.at[target],
            dst_ref=rbuf.at[r, me],
            send_sem=ssem.at[r],
            recv_sem=rsem.at[r],
            device_id={"dom": target},
            device_id_type=MESH,
        ).start()

    def send_far(r):
        def body(j, carry):
            plane = NX * NY - 1 - j
            for dz in DZ_ORDER:
                send(r, peer(lax.rem(plane, NX), dz, plane // NX))
            return carry

        lax.fori_loop(0, NX * NY - 1, body, 0)

    def send_line(r):
        for dz in DZ_ORDER:
            send(r, peer(0, dz, 0))

    def send_plane(r):
        def body(plane, carry):
            send(r, peer(lax.rem(plane, NX), 0, plane // NX))
            return carry

        lax.fori_loop(1, NX * NY, body, 0)

    def receive(r):
        everything = pltpu.make_async_remote_copy(
            src_ref=sbuf.at[pl.ds(0, PEERS - 1)],
            dst_ref=rbuf.at[r, pl.ds(0, PEERS - 1)],
            send_sem=ssem.at[r],
            recv_sem=rsem.at[r],
            device_id={"dom": lax.rem(me + 1, PEERS)},
            device_id_type=MESH,
        )
        everything.wait_send()
        everything.wait_recv()
        got = rbuf[r].astype(F32).reshape(PEERS // 2, 2, 2, 8, 128)
        for h in range(2):
            first, second = swap_pairs(got[:, 0, h], got[:, 1, h])
            halo[:, 256 * h : 256 * h + 128] = first.reshape(SLOTS, 128).astype(BF)
            halo[:, 256 * h + 128 : 256 * h + 256] = second.reshape(SLOTS, 128).astype(BF)

    def tables():
        senders = jnp.transpose(sender_ref[...])
        receivers = jnp.transpose(receiver_ref[...])
        masks = jnp.transpose(mask_ref[...])
        nodes = lax.broadcasted_iota(jnp.int32, (128, NODES), 1)
        slots = lax.broadcasted_iota(jnp.int32, (128, SLOTS), 1)
        node_rows = lax.broadcasted_iota(jnp.int32, (NODES, 128), 0)
        for j in range(EDGES // 128):
            rows = pl.ds(j % 8 * 128, 128)
            mask_col[pl.ds(j * 128, 128), :] = masks[:, j : j + 1].astype(F32)
            received = (receivers[:, j : j + 1] == nodes).astype(BF)
            if j < 8:
                xl[rows, pl.ds(D, NODES)] = received
                xl[rows, pl.ds(D + NODES, NODES)] = (senders[:, j : j + 1] == nodes).astype(BF)
            else:
                xr[rows, pl.ds(D, NODES)] = received
                tr[rows, :] = (senders[:, j : j + 1] - NODES == slots).astype(BF)
            live = jnp.where(mask_ref[j : j + 1, :] > 0, receiver_ref[j : j + 1, :], -1)
            agg_t[:, pl.ds(j * 128, 128)] = (live == node_rows).astype(BF)

    def local_edges(r):
        def body(t, carry):
            rows = pl.ds(pl.multiple_of(t * TILE, TILE), TILE)
            hidden = dot(xl[rows, :], wcat[r]) + bias_ref[r, 0:1, :]
            message, state = edge_tail(
                hidden, xl[rows, pl.ds(0, D)], mask_col[rows, :],
                w_out[r], bias_ref[r], gain_ref[r], shift_ref[r],
            )
            xl[rows, pl.ds(0, D)] = state
            msg[rows, :] = message
            return carry

        lax.fori_loop(0, HALF // TILE, body, 0, unroll=True)
        agg_acc[...] = dot(agg_t[:, pl.ds(0, HALF)], msg[...])

    def remote_start(r):
        def body(t, carry):
            rows = pl.ds(pl.multiple_of(t * TILE, TILE), TILE)
            hpre[rows, :] = dot(xr[rows, :], wcat[r, pl.ds(0, D + NODES), :]) + bias_ref[r, 0:1, :]
            return carry

        lax.fori_loop(0, HALF // TILE, body, 0, unroll=True)

    loads["node"].wait()
    project_and_pack(0)
    pl.semaphore_wait(barrier, NZ - 1 + NX * NY - 1)
    for dz in range(1, NZ):
        tell(ready, peer(0, dz, 0))
    send_line(0)
    load("senders", sender_hbm, sender_ref)
    load("receivers", receiver_hbm, receiver_ref)
    load("masks", mask_hbm, mask_ref)
    load("biases", bias_hbm, bias_ref)
    load("gains", gain_hbm, gain_ref)
    load("shifts", shift_hbm, shift_ref)
    load("recv0", edge_in_hbm.at[0, 2], w_recv.at[0])
    load("edge0", edge_in_hbm.at[0, 0], wcat.at[0, pl.ds(0, D)])
    load("xl", edge_hbm.at[pl.ds(0, HALF)], xl.at[:, pl.ds(0, D)])
    load("out0", edge_out_hbm.at[0], w_out.at[0])
    load("xr", edge_hbm.at[pl.ds(HALF, HALF)], xr.at[:, pl.ds(0, D)])
    load("nin0", node_in_hbm.at[0], n_in.at[0])
    load("nout0", node_out_hbm.at[0], n_out.at[0])
    load("send1", edge_in_hbm.at[1, 1], w_send.at[1])
    load("recv1", edge_in_hbm.at[1, 2], w_recv.at[1])
    load("edge1", edge_in_hbm.at[1, 0], wcat.at[1, pl.ds(0, D)])
    load("out1", edge_out_hbm.at[1], w_out.at[1])
    load("nin1", node_in_hbm.at[1], n_in.at[1])
    load("nout1", node_out_hbm.at[1], n_out.at[1])
    pl.semaphore_wait(ready, NZ - 1)
    send_far(0)
    send_plane(0)
    for name in ("senders", "receivers", "masks", "biases", "gains", "shifts"):
        loads[name].wait()
    tables()

    for r in range(2):
        loads[f"recv{r}"].wait()
        wcat[r, pl.ds(D, NODES), :] = dot(node_state[...], w_recv[r]).astype(BF)
        if r == 0:
            loads["xl"].wait()
            loads["xr"].wait()
        loads[f"edge{r}"].wait()
        loads[f"out{r}"].wait()
        local_edges(r)
        remote_start(r)
        loads[f"nin{r}"].wait()
        loads[f"nout{r}"].wait()
        nh_pre[...] = dot(node_state[...], n_in[r, 0]) + bias_ref[r, 2:3, :]
        receive(r)
        if r == 0:
            remote_edges(
                tr, halo, hpre, xr, mask_col, msg, xr,
                w_out[r], bias_ref[r], gain_ref[r], shift_ref[r],
            )
            node_state[...] = node_step(
                agg_acc, agg_t, msg, nh_pre, node_state,
                n_in[r, 1], n_out[r], bias_ref[r], gain_ref[r], shift_ref[r],
            )
            project_and_pack(1)
            send_far(1)
            send_line(1)
            send_plane(1)


def finish(
    xl, xr, tr, agg_t, hpre, halo, agg_acc, nh_pre, node_state, mask_col,
    w_out, n_in, n_out, bias_ref, gain_ref, shift_ref,
    node_out_hbm, edge_out_hbm,
    msg, state, node_new, osem,
):
    near = pltpu.make_async_copy(xl.at[:, pl.ds(0, D)], edge_out_hbm.at[pl.ds(0, HALF)], osem.at[0])
    near.start()
    remote_edges(
        tr, halo, hpre, xr, mask_col, msg, state,
        w_out[1], bias_ref[1], gain_ref[1], shift_ref[1],
    )
    far = pltpu.make_async_copy(state, edge_out_hbm.at[pl.ds(HALF, HALF)], osem.at[1])
    far.start()
    node_new[...] = node_step(
        agg_acc, agg_t, msg, nh_pre, node_state,
        n_in[1, 1], n_out[1], bias_ref[1], gain_ref[1], shift_ref[1],
    )
    nodes = pltpu.make_async_copy(node_new, node_out_hbm, osem.at[2])
    nodes.start()
    near.wait()
    far.wait()
    nodes.wait()


def local(
    node_latent, edge_latent, edge_sender, edge_receiver, edge_mask, send_list,
    edge_in, edge_out, node_in, node_out, biases, ln_gain, ln_shift,
):
    hbm = pl.BlockSpec(memory_space=pltpu.HBM)
    vmem = pl.BlockSpec(memory_space=pltpu.VMEM)
    args = [
        node_latent, edge_latent,
        edge_sender.reshape(16, 128), edge_receiver.reshape(16, 128), edge_mask.reshape(16, 128),
        send_list.reshape(PEERS, CAP).T,
        edge_in, edge_out, node_in, node_out, biases, ln_gain, ln_shift,
    ]
    held = (
        pltpu.VMEM((HALF, D + 2 * NODES), BF),
        pltpu.VMEM((HALF, D + NODES), BF),
        pltpu.VMEM((HALF, SLOTS), BF),
        pltpu.VMEM((NODES, EDGES), BF),
        pltpu.VMEM((HALF, D), F32),
        pltpu.VMEM((SLOTS, D), BF),
        pltpu.VMEM((NODES, D), F32),
        pltpu.VMEM((NODES, D), F32),
        pltpu.VMEM((NODES, D), BF),
        pltpu.VMEM((EDGES, 1), F32),
        pltpu.VMEM((2, D, D), BF),
        pltpu.VMEM((2, 2, D, D), BF),
        pltpu.VMEM((2, D, D), BF),
        pltpu.VMEM((2, 4, D), F32),
        pltpu.VMEM((2, 2, D), F32),
        pltpu.VMEM((2, 2, D), F32),
    )
    passed = pl.pallas_call(
        kernel,
        out_shape=held,
        in_specs=[hbm] * 13,
        out_specs=(vmem,) * len(held),
        scratch_shapes=[
            pltpu.VMEM((HALF, D), BF),
            pltpu.VMEM((2, D + 2 * NODES, D), BF),
            pltpu.VMEM((2, D, D), BF),
            pltpu.VMEM((2, D, D), BF),
            pltpu.VMEM((SLOTS, NODES), BF),
            pltpu.VMEM((PEERS, 16, 128), BF),
            pltpu.VMEM((2, PEERS, 16, 128), BF),
            pltpu.VMEM((16, 128), jnp.int32),
            pltpu.VMEM((16, 128), jnp.int32),
            pltpu.VMEM((16, 128), jnp.int32),
            pltpu.VMEM((CAP, PEERS), jnp.int32),
            pltpu.SemaphoreType.DMA((2,)),
            pltpu.SemaphoreType.DMA((2,)),
            pltpu.SemaphoreType.REGULAR,
            pltpu.SemaphoreType.DMA((22,)),
        ],
        compiler_params=pltpu.CompilerParams(
            collective_id=0, has_side_effects=True, vmem_limit_bytes=28 * 2**20
        ),
    )(*[pltpu.with_memory_space_constraint(a, pltpu.HBM) for a in args])
    return pl.pallas_call(
        finish,
        out_shape=(pltpu.HBM((NODES, D), BF), pltpu.HBM((EDGES, D), BF)),
        in_specs=[vmem] * len(held),
        out_specs=(hbm, hbm),
        scratch_shapes=[
            pltpu.VMEM((HALF, D), BF),
            pltpu.VMEM((HALF, D), BF),
            pltpu.VMEM((NODES, D), BF),
            pltpu.SemaphoreType.DMA((3,)),
        ],
        compiler_params=pltpu.CompilerParams(vmem_limit_bytes=20 * 2**20),
    )(*passed)


def solution(mesh):
    in_specs = (
        P(("dp", "dom"), None),
        P(("dp", "dom"), None),
        P(("dp", "dom")),
        P(("dp", "dom")),
        P(("dp", "dom")),
        P(("dp", "dom"), None, None),
        P(),
        P(),
        P(),
        P(),
        P(),
        P(),
        P(),
    )
    out_specs = (P(("dp", "dom"), None), P(("dp", "dom"), None))
    return jax.shard_map(local, mesh=mesh, in_specs=in_specs, out_specs=out_specs, check_vma=False)
```

```python
import jax
import jax.numpy as jnp
from jax import lax
from jax.experimental import pallas as pl
from jax.experimental.pallas import tpu as pltpu
from jax.sharding import PartitionSpec as P

MESH = pl.DeviceIdType.MESH
BF = jnp.bfloat16
F32 = jnp.float32

PEERS, CAP, NODES, EDGES, D = 128, 4, 256, 2048, 512
HALF = EDGES // 2
SLOTS = PEERS * CAP
NX, NZ, NY = 4, 8, 4
TILE = 1024
DZ_ORDER = (4, 3, 5, 2, 6, 1, 7)


def dot(a, b):
    return jnp.dot(a, b, preferred_element_type=F32)


def silu(v):
    half = 0.5 * v
    return half * jnp.tanh(half) + half


def layer_norm(values, gain, shift):
    mean = jnp.mean(values, axis=-1, keepdims=True)
    centered = values - mean
    variance = jnp.mean(centered * centered, axis=-1, keepdims=True)
    return centered * lax.rsqrt(variance + 1e-05) * gain + shift


def swap_pairs(even, odd):
    low = lax.broadcasted_iota(jnp.int32, (1, 8, 128), 1) < 4
    first = jnp.where(low, even, pltpu.roll(odd, 4, 1))
    second = jnp.where(low, pltpu.roll(even, 4, 1), odd)
    return first, second


def slot_of(dx, dz, dy):
    plane = dy * NX + dx
    rank = jnp.where(dz < 4, 7 - 2 * dz, 2 * dz - 8)
    near = jnp.where(dz == 0, plane, 16 + plane)
    return jnp.where((dz == 0) | (dz == 4), near, 38 + plane * 6 - rank)


def edge_tail(hidden, state, live, w_out, bias, gain, shift):
    act = silu(hidden).astype(BF)
    projected = dot(act, w_out) + bias[1:2, :]
    message = layer_norm(projected, gain[0:1, :], shift[0:1, :])
    message = jnp.where(live > 0, message, 0.0).astype(BF)
    return message, state + message


def remote_edges(tr, halo, hpre, xr, mask_col, agg_t, agg_acc, state_ref, w_out, bias, gain, shift):
    total = agg_acc[...]
    for t in range(HALF // TILE):
        rows, later = pl.ds(t * TILE, TILE), pl.ds(HALF + t * TILE, TILE)
        hidden = dot(tr[rows, pl.ds(0, SLOTS // 2)], halo[pl.ds(0, SLOTS // 2), :]) + hpre[rows, :]
        message, state = edge_tail(
            hidden, xr[rows, pl.ds(0, D)], mask_col[later, :], w_out, bias, gain, shift
        )
        state_ref[rows, pl.ds(0, D)] = state
        total = total + dot(agg_t[:, later], message)
    return total.astype(BF)


def node_step(total, nh_pre, node_state, w_in, w_out, bias, gain, shift):
    act = silu(nh_pre[...] + dot(total, w_in)).astype(BF)
    projected = dot(act, w_out) + bias[3:4, :]
    update = layer_norm(projected, gain[1:2, :], shift[1:2, :])
    return (node_state[...].astype(F32) + update).astype(BF)


def kernel(
    node_hbm, edge_hbm, sender_hbm, receiver_hbm, mask_hbm, list_hbm,
    edge_in_hbm, edge_out_hbm, node_in_hbm, node_out_hbm, bias_hbm, gain_hbm, shift_hbm,
    xl, xr, tr, agg_t, hpre, halo, agg_acc, nh_pre, node_state, mask_col,
    w_out, n_in, n_out, bias_ref, gain_ref, shift_ref,
    wcat, w_send, w_recv, pick, sbuf, rbuf, bundled,
    sender_ref, receiver_ref, mask_ref, list_ref,
    ssem, rsem, bsem, ready, lsem,
):
    me = lax.axis_index("dom")
    x, z, y = lax.rem(me, NX), lax.rem(me // NX, NZ), me // (NX * NZ)

    def peer(dx, dz, dy):
        return (lax.rem(y + dy, NY) * NZ + lax.rem(z + dz, NZ)) * NX + lax.rem(x + dx, NX)

    def tell(sem, target):
        pl.semaphore_signal(sem, inc=1, device_id={"dom": target}, device_id_type=MESH)

    loads = {}

    def load(name, src, dst):
        copy = pltpu.make_async_copy(src, dst, lsem.at[len(loads)])
        copy.start()
        loads[name] = copy

    load("list", list_hbm, list_ref)
    load("node", node_hbm, node_state)
    load("send0", edge_in_hbm.at[0, 1], w_send.at[0])

    barrier = pltpu.get_barrier_semaphore()
    for plane in range(1, NX * NY):
        tell(barrier, peer(plane % NX, 0, plane // NX))
    for dz in range(1, NZ):
        tell(barrier, peer(0, dz, 0))

    p = lax.broadcasted_iota(jnp.int32, (1, PEERS), 1)
    to = slot_of((p - x) & (NX - 1), ((p >> 2) - z) & (NZ - 1), ((p >> 5) - y) & (NY - 1))
    spread = (lax.broadcasted_iota(jnp.int32, (SLOTS, PEERS), 0) // CAP == to).astype(BF)
    loads["list"].wait()
    lists = lax.dot_general(
        spread, list_ref[...].astype(F32).astype(BF), (((1,), (1,)), ((), ())), preferred_element_type=F32
    )
    own = lax.broadcasted_iota(jnp.int32, (SLOTS, CAP), 0) % CAP == lax.broadcasted_iota(
        jnp.int32, (SLOTS, CAP), 1
    )
    chosen = jnp.sum(jnp.where(own, lists, 0.0), axis=1, keepdims=True).astype(jnp.int32)
    pick[...] = (chosen == lax.broadcasted_iota(jnp.int32, (SLOTS, NODES), 1)).astype(BF)
    for r in range(2):
        rbuf[r, 0] = jnp.zeros((16, 128), BF)

    def project_and_pack(r):
        loads[f"send{r}"].wait()
        send_proj = dot(node_state[...], w_send[r]).astype(BF)
        wcat[r, pl.ds(D + NODES, NODES), :] = send_proj
        rows = dot(pick[...], send_proj)
        for h in range(2):
            first, second = swap_pairs(
                rows[:, 256 * h : 256 * h + 128].reshape(PEERS // 2, 8, 128),
                rows[:, 256 * h + 128 : 256 * h + 256].reshape(PEERS // 2, 8, 128),
            )
            part = jnp.stack([first, second], axis=1).reshape(PEERS, 8, 128)
            if h == 0:
                upper = part
        sbuf[...] = jnp.concatenate([upper, part], axis=1).astype(BF)

    def send(r, group, slot, target):
        pltpu.make_async_remote_copy(
            src_ref=sbuf.at[slot],
            dst_ref=rbuf.at[r, slot],
            send_sem=ssem.at[r],
            recv_sem=rsem.at[r, group],
            device_id={"dom": target},
            device_id_type=MESH,
        ).start()

    def send_off_plane(r, group, plane, ranks, opposite):
        if opposite:
            send(r, 1, 16 + plane, peer(lax.rem(plane, NX), 4, plane // NX))
        for rank in ranks:
            send(r, group, 38 + plane * 6 - rank, peer(lax.rem(plane, NX), DZ_ORDER[rank], plane // NX))

    def send_far(r):
        def first(j, carry):
            send_off_plane(r, 0, 15 - j, range(1, 7), r == 1)
            return carry

        def second(j, carry):
            send_off_plane(r, 1, 4 - j, range(1, 7), r == 1)
            return carry

        lax.fori_loop(0, 10, first, 0)
        send_off_plane(r, 0, 5, range(1, 5), r == 1)
        send_off_plane(r, 1, 5, range(5, 7), False)
        lax.fori_loop(0, 4, second, 0)

    def send_line(r):
        send_off_plane(r, 1, 0, range(1, 7), r == 1)

    def bundle():
        return pltpu.make_async_remote_copy(
            src_ref=sbuf.at[pl.ds(16, 16)],
            dst_ref=bundled,
            send_sem=bsem.at[0],
            recv_sem=bsem.at[1],
            device_id={"dom": peer(0, 4, 0)},
            device_id_type=MESH,
        )

    def forward(plane):
        return pltpu.make_async_remote_copy(
            src_ref=bundled.at[plane],
            dst_ref=rbuf.at[0, 16 + plane],
            send_sem=bsem.at[2],
            recv_sem=rsem.at[0, 1],
            device_id={"dom": peer(lax.rem(plane, NX), 0, plane // NX)},
            device_id_type=MESH,
        )

    def forward_bundle():
        bundle().wait()

        def body(plane, carry):
            forward(plane).start()
            return carry

        lax.fori_loop(1, NX * NY, body, 0)
        rbuf[0, 16] = bundled[0]

    def send_plane(r):
        def body(plane, carry):
            send(r, 1, plane, peer(lax.rem(plane, NX), 0, plane // NX))
            return carry

        lax.fori_loop(1, NX * NY, body, 0)

    def arrived(r, first, count, group):
        return pltpu.make_async_remote_copy(
            src_ref=sbuf.at[pl.ds(first, count)],
            dst_ref=rbuf.at[r, pl.ds(first, count)],
            send_sem=ssem.at[r],
            recv_sem=rsem.at[r, group],
            device_id={"dom": lax.rem(me + 1, PEERS)},
            device_id_type=MESH,
        )

    def receive(r, group):
        if group == 0:
            arrived(r, 64, 64, 0).wait_recv()
        else:
            arrived(r, 1, 63 - (r == 0), 1).wait_recv()
        first, rows = (1 - group) * 64, SLOTS // 2
        got = rbuf[r, pl.ds(first, 64)].astype(F32).reshape(32, 2, 2, 8, 128)
        for h in range(2):
            left, right = swap_pairs(got[:, 0, h], got[:, 1, h])
            at = pl.ds(first * CAP, rows)
            halo[at, 256 * h : 256 * h + 128] = left.reshape(rows, 128).astype(BF)
            halo[at, 256 * h + 128 : 256 * h + 256] = right.reshape(rows, 128).astype(BF)

    def remote_half(r):
        for t in range(HALF // TILE):
            rows, late = pl.ds(t * TILE, TILE), pl.ds(SLOTS // 2, SLOTS // 2)
            hpre[rows, :] = hpre[rows, :] + dot(tr[rows, late], halo[late, :])

    def tables():
        far = sender_ref[...] - NODES
        at = slot_of(
            (x - (far >> 2)) & (NX - 1), (z - (far >> 4)) & (NZ - 1), (y - (far >> 7)) & (NY - 1)
        )
        senders = jnp.transpose(jnp.where(far >= 0, at * CAP + (far & (CAP - 1)), sender_ref[...]))
        receivers = jnp.transpose(receiver_ref[...])
        masks = jnp.transpose(mask_ref[...])
        nodes = lax.broadcasted_iota(jnp.int32, (128, NODES), 1)
        slots = lax.broadcasted_iota(jnp.int32, (128, SLOTS), 1)
        node_rows = lax.broadcasted_iota(jnp.int32, (NODES, 128), 0)
        for j in range(EDGES // 128):
            rows = pl.ds(j % 8 * 128, 128)
            mask_col[pl.ds(j * 128, 128), :] = masks[:, j : j + 1].astype(F32)
            received = (receivers[:, j : j + 1] == nodes).astype(BF)
            if j < 8:
                xl[rows, pl.ds(D, NODES)] = received
                xl[rows, pl.ds(D + NODES, NODES)] = (senders[:, j : j + 1] == nodes).astype(BF)
            else:
                xr[rows, pl.ds(D, NODES)] = received
                tr[rows, :] = (senders[:, j : j + 1] == slots).astype(BF)
            live = jnp.where(mask_ref[j : j + 1, :] > 0, receiver_ref[j : j + 1, :], -1)
            agg_t[:, pl.ds(j * 128, 128)] = (live == node_rows).astype(BF)

    def local_edges(r):
        total = jnp.zeros((NODES, D), F32)
        for t in range(HALF // TILE):
            rows = pl.ds(t * TILE, TILE)
            hidden = dot(xl[rows, :], wcat[r]) + bias_ref[r, 0:1, :]
            message, state = edge_tail(
                hidden, xl[rows, pl.ds(0, D)], mask_col[rows, :],
                w_out[r], bias_ref[r], gain_ref[r], shift_ref[r],
            )
            xl[rows, pl.ds(0, D)] = state
            total = total + dot(agg_t[:, rows], message)
        agg_acc[...] = total

    def remote_start(r):
        for t in range(HALF // TILE):
            rows = pl.ds(t * TILE, TILE)
            hpre[rows, :] = dot(xr[rows, :], wcat[r, pl.ds(0, D + NODES), :]) + bias_ref[r, 0:1, :]

    loads["node"].wait()
    project_and_pack(0)
    pl.semaphore_wait(barrier, NZ - 1 + NX * NY - 1)
    for dz in range(1, NZ):
        tell(ready, peer(0, dz, 0))
    bundle().start()
    send_line(0)
    load("senders", sender_hbm, sender_ref)
    load("receivers", receiver_hbm, receiver_ref)
    load("masks", mask_hbm, mask_ref)
    load("biases", bias_hbm, bias_ref)
    load("gains", gain_hbm, gain_ref)
    load("shifts", shift_hbm, shift_ref)
    load("recv0", edge_in_hbm.at[0, 2], w_recv.at[0])
    load("edge0", edge_in_hbm.at[0, 0], wcat.at[0, pl.ds(0, D)])
    load("xl", edge_hbm.at[pl.ds(0, HALF)], xl.at[:, pl.ds(0, D)])
    load("out0", edge_out_hbm.at[0], w_out.at[0])
    load("xr", edge_hbm.at[pl.ds(HALF, HALF)], xr.at[:, pl.ds(0, D)])
    load("nin0", node_in_hbm.at[0], n_in.at[0])
    load("nout0", node_out_hbm.at[0], n_out.at[0])
    load("send1", edge_in_hbm.at[1, 1], w_send.at[1])
    load("recv1", edge_in_hbm.at[1, 2], w_recv.at[1])
    load("edge1", edge_in_hbm.at[1, 0], wcat.at[1, pl.ds(0, D)])
    load("out1", edge_out_hbm.at[1], w_out.at[1])
    load("nin1", node_in_hbm.at[1], n_in.at[1])
    load("nout1", node_out_hbm.at[1], n_out.at[1])
    pl.semaphore_wait(ready, NZ - 1)
    send_far(0)
    forward_bundle()
    send_plane(0)
    for name in ("senders", "receivers", "masks", "biases", "gains", "shifts"):
        loads[name].wait()
    tables()

    for r in range(2):
        loads[f"recv{r}"].wait()
        wcat[r, pl.ds(D, NODES), :] = dot(node_state[...], w_recv[r]).astype(BF)
        if r == 0:
            loads["xl"].wait()
            loads["xr"].wait()
        loads[f"edge{r}"].wait()
        loads[f"out{r}"].wait()
        local_edges(r)
        remote_start(r)
        loads[f"nin{r}"].wait()
        loads[f"nout{r}"].wait()
        nh_pre[...] = dot(node_state[...], n_in[r, 0]) + bias_ref[r, 2:3, :]
        receive(r, 0)
        remote_half(r)
        arrived(r, 0, 111 if r == 0 else 127, 0).wait_send()
        if r == 0:
            pltpu.make_async_remote_copy(
                src_ref=bundled.at[pl.ds(1, 15)],
                dst_ref=rbuf.at[0, pl.ds(1, 15)],
                send_sem=bsem.at[2],
                recv_sem=rsem.at[0, 1],
                device_id={"dom": lax.rem(me + 1, PEERS)},
                device_id_type=MESH,
            ).wait_send()
        receive(r, 1)
        if r == 0:
            total = remote_edges(
                tr, halo, hpre, xr, mask_col, agg_t, agg_acc, xr,
                w_out[r], bias_ref[r], gain_ref[r], shift_ref[r],
            )
            node_state[...] = node_step(
                total, nh_pre, node_state,
                n_in[r, 1], n_out[r], bias_ref[r], gain_ref[r], shift_ref[r],
            )
            project_and_pack(1)
            send_far(1)
            send_line(1)
            send_plane(1)


def finish(
    xl, xr, tr, agg_t, hpre, halo, agg_acc, nh_pre, node_state, mask_col,
    w_out, n_in, n_out, bias_ref, gain_ref, shift_ref,
    node_out_hbm, edge_out_hbm,
    state, node_new, osem,
):
    near = pltpu.make_async_copy(xl.at[:, pl.ds(0, D)], edge_out_hbm.at[pl.ds(0, HALF)], osem.at[0])
    near.start()
    total = remote_edges(
        tr, halo, hpre, xr, mask_col, agg_t, agg_acc, state,
        w_out[1], bias_ref[1], gain_ref[1], shift_ref[1],
    )
    far = pltpu.make_async_copy(state, edge_out_hbm.at[pl.ds(HALF, HALF)], osem.at[1])
    far.start()
    node_new[...] = node_step(
        total, nh_pre, node_state,
        n_in[1, 1], n_out[1], bias_ref[1], gain_ref[1], shift_ref[1],
    )
    nodes = pltpu.make_async_copy(node_new, node_out_hbm, osem.at[2])
    nodes.start()
    near.wait()
    far.wait()
    nodes.wait()


def local(
    node_latent, edge_latent, edge_sender, edge_receiver, edge_mask, send_list,
    edge_in, edge_out, node_in, node_out, biases, ln_gain, ln_shift,
):
    hbm = pl.BlockSpec(memory_space=pltpu.HBM)
    vmem = pl.BlockSpec(memory_space=pltpu.VMEM)
    args = [
        node_latent, edge_latent,
        edge_sender.reshape(16, 128), edge_receiver.reshape(16, 128), edge_mask.reshape(16, 128),
        send_list.reshape(PEERS, CAP).T,
        edge_in, edge_out, node_in, node_out, biases, ln_gain, ln_shift,
    ]
    held = (
        pltpu.VMEM((HALF, D + 2 * NODES), BF),
        pltpu.VMEM((HALF, D + NODES), BF),
        pltpu.VMEM((HALF, SLOTS), BF),
        pltpu.VMEM((NODES, EDGES), BF),
        pltpu.VMEM((HALF, D), F32),
        pltpu.VMEM((SLOTS, D), BF),
        pltpu.VMEM((NODES, D), F32),
        pltpu.VMEM((NODES, D), F32),
        pltpu.VMEM((NODES, D), BF),
        pltpu.VMEM((EDGES, 1), F32),
        pltpu.VMEM((2, D, D), BF),
        pltpu.VMEM((2, 2, D, D), BF),
        pltpu.VMEM((2, D, D), BF),
        pltpu.VMEM((2, 4, D), F32),
        pltpu.VMEM((2, 2, D), F32),
        pltpu.VMEM((2, 2, D), F32),
    )
    passed = pl.pallas_call(
        kernel,
        out_shape=held,
        in_specs=[hbm] * 13,
        out_specs=(vmem,) * len(held),
        scratch_shapes=[
            pltpu.VMEM((2, D + 2 * NODES, D), BF),
            pltpu.VMEM((2, D, D), BF),
            pltpu.VMEM((2, D, D), BF),
            pltpu.VMEM((SLOTS, NODES), BF),
            pltpu.VMEM((PEERS, 16, 128), BF),
            pltpu.VMEM((2, PEERS, 16, 128), BF),
            pltpu.VMEM((16, 16, 128), BF),
            pltpu.VMEM((16, 128), jnp.int32),
            pltpu.VMEM((16, 128), jnp.int32),
            pltpu.VMEM((16, 128), jnp.int32),
            pltpu.VMEM((CAP, PEERS), jnp.int32),
            pltpu.SemaphoreType.DMA((2,)),
            pltpu.SemaphoreType.DMA((2, 2)),
            pltpu.SemaphoreType.DMA((3,)),
            pltpu.SemaphoreType.REGULAR,
            pltpu.SemaphoreType.DMA((22,)),
        ],
        compiler_params=pltpu.CompilerParams(
            collective_id=0, has_side_effects=True, vmem_limit_bytes=28 * 2**20
        ),
    )(*[pltpu.with_memory_space_constraint(a, pltpu.HBM) for a in args])
    return pl.pallas_call(
        finish,
        out_shape=(pltpu.HBM((NODES, D), BF), pltpu.HBM((EDGES, D), BF)),
        in_specs=[vmem] * len(held),
        out_specs=(hbm, hbm),
        scratch_shapes=[
            pltpu.VMEM((HALF, D), BF),
            pltpu.VMEM((NODES, D), BF),
            pltpu.SemaphoreType.DMA((3,)),
        ],
        compiler_params=pltpu.CompilerParams(vmem_limit_bytes=20 * 2**20),
    )(*passed)


def solution(mesh):
    in_specs = (
        P(("dp", "dom"), None),
        P(("dp", "dom"), None),
        P(("dp", "dom")),
        P(("dp", "dom")),
        P(("dp", "dom")),
        P(("dp", "dom"), None, None),
        P(),
        P(),
        P(),
        P(),
        P(),
        P(),
        P(),
    )
    out_specs = (P(("dp", "dom"), None), P(("dp", "dom"), None))
    return jax.shard_map(local, mesh=mesh, in_specs=in_specs, out_specs=out_specs, check_vma=False)
```

```python
import jax
import jax.numpy as jnp
from jax import lax
from jax.experimental import pallas as pl
from jax.experimental.pallas import tpu as pltpu
from jax.sharding import PartitionSpec as P

MESH = pl.DeviceIdType.MESH
BF = jnp.bfloat16
F32 = jnp.float32

PEERS, CAP, NODES, EDGES, D = 128, 4, 256, 2048, 512
HALF = EDGES // 2
SLOTS = PEERS * CAP
NX, NZ, NY = 4, 8, 4
TILE = 1024
DZ_ORDER = (4, 3, 5, 2, 6, 1, 7)


def dot(a, b):
    return jnp.dot(a, b, preferred_element_type=F32)


def silu(v):
    half = 0.5 * v
    return half * jnp.tanh(half) + half


def layer_norm(values, gain, shift):
    mean = jnp.mean(values, axis=-1, keepdims=True)
    centered = values - mean
    variance = jnp.mean(centered * centered, axis=-1, keepdims=True)
    return centered * lax.rsqrt(variance + 1e-05) * gain + shift


def swap_pairs(even, odd):
    low = lax.broadcasted_iota(jnp.int32, (1, 8, 128), 1) < 4
    first = jnp.where(low, even, pltpu.roll(odd, 4, 1))
    second = jnp.where(low, pltpu.roll(even, 4, 1), odd)
    return first, second


def slot_of(dx, dz, dy):
    plane = dy * NX + dx
    rank = jnp.where(dz < 4, 7 - 2 * dz, 2 * dz - 8)
    near = jnp.where(dz == 0, plane, 16 + plane)
    return jnp.where((dz == 0) | (dz == 4), near, 38 + plane * 6 - rank)


def edge_tail(hidden, state, live, w_out, bias, gain, shift):
    act = silu(hidden).astype(BF)
    projected = dot(act, w_out) + bias[1:2, :]
    message = layer_norm(projected, gain[0:1, :], shift[0:1, :])
    message = jnp.where(live > 0, message, 0.0).astype(BF)
    return message, state + message


def remote_edges(tr, halo, hpre, xr, mask_col, agg_t, agg_acc, state_ref, w_out, bias, gain, shift):
    total = agg_acc[...]
    for t in range(HALF // TILE):
        rows, later = pl.ds(t * TILE, TILE), pl.ds(HALF + t * TILE, TILE)
        hidden = dot(tr[rows, pl.ds(0, SLOTS // 2)], halo[pl.ds(0, SLOTS // 2), :]) + hpre[rows, :]
        message, state = edge_tail(
            hidden, xr[rows, pl.ds(0, D)], mask_col[later, :], w_out, bias, gain, shift
        )
        state_ref[rows, pl.ds(0, D)] = state
        total = total + dot(agg_t[:, later], message)
    return total.astype(BF)


def node_step(total, nh_pre, node_state, w_in, w_out, bias, gain, shift):
    act = silu(nh_pre[...] + dot(total, w_in)).astype(BF)
    projected = dot(act, w_out) + bias[3:4, :]
    update = layer_norm(projected, gain[1:2, :], shift[1:2, :])
    return (node_state[...].astype(F32) + update).astype(BF)


def kernel(
    node_hbm, edge_hbm, sender_hbm, receiver_hbm, mask_hbm, list_hbm,
    edge_in_hbm, edge_out_hbm, node_in_hbm, node_out_hbm, bias_hbm, gain_hbm, shift_hbm,
    xl, xr, tr, agg_t, hpre, halo, agg_acc, nh_pre, node_state, mask_col,
    w_out, n_in, n_out, bias_ref, gain_ref, shift_ref,
    wcat, w_send, w_recv, pick, sbuf, rbuf, bundled,
    sender_ref, receiver_ref, mask_ref, list_ref,
    ssem, rsem, bsem, ready, lsem,
):
    me = lax.axis_index("dom")
    x, z, y = lax.rem(me, NX), lax.rem(me // NX, NZ), me // (NX * NZ)

    def peer(dx, dz, dy):
        return (lax.rem(y + dy, NY) * NZ + lax.rem(z + dz, NZ)) * NX + lax.rem(x + dx, NX)

    def tell(sem, target):
        pl.semaphore_signal(sem, inc=1, device_id={"dom": target}, device_id_type=MESH)

    loads = {}

    def load(name, src, dst):
        copy = pltpu.make_async_copy(src, dst, lsem.at[len(loads)])
        copy.start()
        loads[name] = copy

    load("list", list_hbm, list_ref)
    load("node", node_hbm, node_state)
    load("send0", edge_in_hbm.at[0, 1], w_send.at[0])
    load("senders", sender_hbm, sender_ref)
    load("receivers", receiver_hbm, receiver_ref)
    load("masks", mask_hbm, mask_ref)

    barrier = pltpu.get_barrier_semaphore()
    for plane in range(1, NX * NY):
        tell(barrier, peer(plane % NX, 0, plane // NX))
    for dz in range(1, NZ):
        tell(barrier, peer(0, dz, 0))

    p = lax.broadcasted_iota(jnp.int32, (1, PEERS), 1)
    to = slot_of((p - x) & (NX - 1), ((p >> 2) - z) & (NZ - 1), ((p >> 5) - y) & (NY - 1))
    spread = (lax.broadcasted_iota(jnp.int32, (SLOTS, PEERS), 0) // CAP == to).astype(BF)
    loads["list"].wait()
    lists = lax.dot_general(
        spread, list_ref[...].astype(F32).astype(BF), (((1,), (1,)), ((), ())), preferred_element_type=F32
    )
    own = lax.broadcasted_iota(jnp.int32, (SLOTS, CAP), 0) % CAP == lax.broadcasted_iota(
        jnp.int32, (SLOTS, CAP), 1
    )
    chosen = jnp.sum(jnp.where(own, lists, 0.0), axis=1, keepdims=True).astype(jnp.int32)
    pick[...] = (chosen == lax.broadcasted_iota(jnp.int32, (SLOTS, NODES), 1)).astype(BF)
    for r in range(2):
        rbuf[r, 0] = jnp.zeros((16, 128), BF)

    def project_and_pack(r):
        loads[f"send{r}"].wait()
        send_proj = dot(node_state[...], w_send[r]).astype(BF)
        wcat[r, pl.ds(D + NODES, NODES), :] = send_proj
        rows = dot(pick[...], send_proj)
        for h in range(2):
            first, second = swap_pairs(
                rows[:, 256 * h : 256 * h + 128].reshape(PEERS // 2, 8, 128),
                rows[:, 256 * h + 128 : 256 * h + 256].reshape(PEERS // 2, 8, 128),
            )
            part = jnp.stack([first, second], axis=1).reshape(PEERS, 8, 128)
            if h == 0:
                upper = part
        sbuf[...] = jnp.concatenate([upper, part], axis=1).astype(BF)

    def send(r, group, slot, target):
        pltpu.make_async_remote_copy(
            src_ref=sbuf.at[slot],
            dst_ref=rbuf.at[r, slot],
            send_sem=ssem.at[r],
            recv_sem=rsem.at[r, group],
            device_id={"dom": target},
            device_id_type=MESH,
        ).start()

    def send_off_plane(r, group, plane, ranks, opposite):
        if opposite:
            send(r, 1, 16 + plane, peer(lax.rem(plane, NX), 4, plane // NX))
        for rank in ranks:
            send(r, group, 38 + plane * 6 - rank, peer(lax.rem(plane, NX), DZ_ORDER[rank], plane // NX))

    def send_far(r):
        def first(j, carry):
            send_off_plane(r, 0, 15 - j, range(1, 7), r == 1)
            return carry

        def second(j, carry):
            send_off_plane(r, 1, 4 - j, range(1, 7), r == 1)
            return carry

        lax.fori_loop(0, 10, first, 0)
        send_off_plane(r, 0, 5, range(1, 5), r == 1)
        send_off_plane(r, 1, 5, range(5, 7), False)
        lax.fori_loop(0, 4, second, 0)

    def send_line(r):
        send_off_plane(r, 1, 0, range(1, 7), r == 1)

    def bundle():
        return pltpu.make_async_remote_copy(
            src_ref=sbuf.at[pl.ds(16, 16)],
            dst_ref=bundled,
            send_sem=bsem.at[0],
            recv_sem=bsem.at[1],
            device_id={"dom": peer(0, 4, 0)},
            device_id_type=MESH,
        )

    def forward(plane):
        return pltpu.make_async_remote_copy(
            src_ref=bundled.at[plane],
            dst_ref=rbuf.at[0, 16 + plane],
            send_sem=bsem.at[2],
            recv_sem=rsem.at[0, 1],
            device_id={"dom": peer(lax.rem(plane, NX), 0, plane // NX)},
            device_id_type=MESH,
        )

    def forward_bundle():
        bundle().wait()

        def body(plane, carry):
            forward(plane).start()
            return carry

        lax.fori_loop(1, NX * NY, body, 0)
        rbuf[0, 16] = bundled[0]

    def send_plane(r):
        def body(plane, carry):
            send(r, 1, plane, peer(lax.rem(plane, NX), 0, plane // NX))
            return carry

        lax.fori_loop(1, NX * NY, body, 0)

    def arrived(r, first, count, group):
        return pltpu.make_async_remote_copy(
            src_ref=sbuf.at[pl.ds(first, count)],
            dst_ref=rbuf.at[r, pl.ds(first, count)],
            send_sem=ssem.at[r],
            recv_sem=rsem.at[r, group],
            device_id={"dom": lax.rem(me + 1, PEERS)},
            device_id_type=MESH,
        )

    def receive(r, group):
        if group == 0:
            arrived(r, 64, 64, 0).wait_recv()
        else:
            arrived(r, 1, 63 - (r == 0), 1).wait_recv()
        first, rows = (1 - group) * 64, SLOTS // 2
        got = rbuf[r, pl.ds(first, 64)].astype(F32).reshape(32, 2, 2, 8, 128)
        for h in range(2):
            left, right = swap_pairs(got[:, 0, h], got[:, 1, h])
            at = pl.ds(first * CAP, rows)
            halo[at, 256 * h : 256 * h + 128] = left.reshape(rows, 128).astype(BF)
            halo[at, 256 * h + 128 : 256 * h + 256] = right.reshape(rows, 128).astype(BF)

    def remote_half(r):
        for t in range(HALF // TILE):
            rows, late = pl.ds(t * TILE, TILE), pl.ds(SLOTS // 2, SLOTS // 2)
            hpre[rows, :] = hpre[rows, :] + dot(tr[rows, late], halo[late, :])

    def tables():
        far = sender_ref[...] - NODES
        at = slot_of(
            (x - (far >> 2)) & (NX - 1), (z - (far >> 4)) & (NZ - 1), (y - (far >> 7)) & (NY - 1)
        )
        senders = jnp.transpose(jnp.where(far >= 0, at * CAP + (far & (CAP - 1)), sender_ref[...]))
        receivers = jnp.transpose(receiver_ref[...])
        masks = jnp.transpose(mask_ref[...])
        nodes = lax.broadcasted_iota(jnp.int32, (128, NODES), 1)
        slots = lax.broadcasted_iota(jnp.int32, (128, SLOTS), 1)
        node_rows = lax.broadcasted_iota(jnp.int32, (NODES, 128), 0)
        for j in range(EDGES // 128):
            rows = pl.ds(j % 8 * 128, 128)
            mask_col[pl.ds(j * 128, 128), :] = masks[:, j : j + 1].astype(F32)
            received = (receivers[:, j : j + 1] == nodes).astype(BF)
            if j < 8:
                xl[rows, pl.ds(D, NODES)] = received
                xl[rows, pl.ds(D + NODES, NODES)] = (senders[:, j : j + 1] == nodes).astype(BF)
            else:
                xr[rows, pl.ds(D, NODES)] = received
                tr[rows, :] = (senders[:, j : j + 1] == slots).astype(BF)
            live = jnp.where(mask_ref[j : j + 1, :] > 0, receiver_ref[j : j + 1, :], -1)
            agg_t[:, pl.ds(j * 128, 128)] = (live == node_rows).astype(BF)

    def local_edges(r):
        total = jnp.zeros((NODES, D), F32)
        for t in range(HALF // TILE):
            rows = pl.ds(t * TILE, TILE)
            hidden = dot(xl[rows, :], wcat[r]) + bias_ref[r, 0:1, :]
            message, state = edge_tail(
                hidden, xl[rows, pl.ds(0, D)], mask_col[rows, :],
                w_out[r], bias_ref[r], gain_ref[r], shift_ref[r],
            )
            xl[rows, pl.ds(0, D)] = state
            total = total + dot(agg_t[:, rows], message)
        agg_acc[...] = total

    def remote_start(r):
        for t in range(HALF // TILE):
            rows = pl.ds(t * TILE, TILE)
            hpre[rows, :] = dot(xr[rows, :], wcat[r, pl.ds(0, D + NODES), :]) + bias_ref[r, 0:1, :]

    loads["node"].wait()
    project_and_pack(0)
    pl.semaphore_wait(barrier, NZ - 1 + NX * NY - 1)
    for dz in range(1, NZ):
        tell(ready, peer(0, dz, 0))
    bundle().start()
    send_line(0)
    load("biases", bias_hbm, bias_ref)
    load("gains", gain_hbm, gain_ref)
    load("shifts", shift_hbm, shift_ref)
    load("recv0", edge_in_hbm.at[0, 2], w_recv.at[0])
    load("edge0", edge_in_hbm.at[0, 0], wcat.at[0, pl.ds(0, D)])
    load("xl", edge_hbm.at[pl.ds(0, HALF)], xl.at[:, pl.ds(0, D)])
    load("out0", edge_out_hbm.at[0], w_out.at[0])
    load("xr", edge_hbm.at[pl.ds(HALF, HALF)], xr.at[:, pl.ds(0, D)])
    load("nin0", node_in_hbm.at[0], n_in.at[0])
    load("nout0", node_out_hbm.at[0], n_out.at[0])
    load("send1", edge_in_hbm.at[1, 1], w_send.at[1])
    load("recv1", edge_in_hbm.at[1, 2], w_recv.at[1])
    load("edge1", edge_in_hbm.at[1, 0], wcat.at[1, pl.ds(0, D)])
    load("out1", edge_out_hbm.at[1], w_out.at[1])
    load("nin1", node_in_hbm.at[1], n_in.at[1])
    load("nout1", node_out_hbm.at[1], n_out.at[1])
    for name in ("senders", "receivers", "masks"):
        loads[name].wait()
    tables()
    pl.semaphore_wait(ready, NZ - 1)
    send_far(0)
    forward_bundle()
    send_plane(0)
    for name in ("biases", "gains", "shifts"):
        loads[name].wait()

    for r in range(2):
        loads[f"recv{r}"].wait()
        wcat[r, pl.ds(D, NODES), :] = dot(node_state[...], w_recv[r]).astype(BF)
        if r == 0:
            loads["xl"].wait()
            loads["xr"].wait()
        loads[f"edge{r}"].wait()
        loads[f"out{r}"].wait()
        local_edges(r)
        remote_start(r)
        loads[f"nin{r}"].wait()
        loads[f"nout{r}"].wait()
        nh_pre[...] = dot(node_state[...], n_in[r, 0]) + bias_ref[r, 2:3, :]
        receive(r, 0)
        remote_half(r)
        arrived(r, 0, 111 if r == 0 else 127, 0).wait_send()
        if r == 0:
            pltpu.make_async_remote_copy(
                src_ref=bundled.at[pl.ds(1, 15)],
                dst_ref=rbuf.at[0, pl.ds(1, 15)],
                send_sem=bsem.at[2],
                recv_sem=rsem.at[0, 1],
                device_id={"dom": lax.rem(me + 1, PEERS)},
                device_id_type=MESH,
            ).wait_send()
        receive(r, 1)
        if r == 0:
            total = remote_edges(
                tr, halo, hpre, xr, mask_col, agg_t, agg_acc, xr,
                w_out[r], bias_ref[r], gain_ref[r], shift_ref[r],
            )
            node_state[...] = node_step(
                total, nh_pre, node_state,
                n_in[r, 1], n_out[r], bias_ref[r], gain_ref[r], shift_ref[r],
            )
            project_and_pack(1)
            send_far(1)
            send_line(1)
            send_plane(1)


def finish(
    xl, xr, tr, agg_t, hpre, halo, agg_acc, nh_pre, node_state, mask_col,
    w_out, n_in, n_out, bias_ref, gain_ref, shift_ref,
    node_out_hbm, edge_out_hbm,
    state, node_new, osem,
):
    near = pltpu.make_async_copy(xl.at[:, pl.ds(0, D)], edge_out_hbm.at[pl.ds(0, HALF)], osem.at[0])
    near.start()
    total = remote_edges(
        tr, halo, hpre, xr, mask_col, agg_t, agg_acc, state,
        w_out[1], bias_ref[1], gain_ref[1], shift_ref[1],
    )
    far = pltpu.make_async_copy(state, edge_out_hbm.at[pl.ds(HALF, HALF)], osem.at[1])
    far.start()
    node_new[...] = node_step(
        total, nh_pre, node_state,
        n_in[1, 1], n_out[1], bias_ref[1], gain_ref[1], shift_ref[1],
    )
    nodes = pltpu.make_async_copy(node_new, node_out_hbm, osem.at[2])
    nodes.start()
    near.wait()
    far.wait()
    nodes.wait()


def local(
    node_latent, edge_latent, edge_sender, edge_receiver, edge_mask, send_list,
    edge_in, edge_out, node_in, node_out, biases, ln_gain, ln_shift,
):
    hbm = pl.BlockSpec(memory_space=pltpu.HBM)
    vmem = pl.BlockSpec(memory_space=pltpu.VMEM)
    args = [
        node_latent, edge_latent,
        edge_sender.reshape(16, 128), edge_receiver.reshape(16, 128), edge_mask.reshape(16, 128),
        send_list.reshape(PEERS, CAP).T,
        edge_in, edge_out, node_in, node_out, biases, ln_gain, ln_shift,
    ]
    held = (
        pltpu.VMEM((HALF, D + 2 * NODES), BF),
        pltpu.VMEM((HALF, D + NODES), BF),
        pltpu.VMEM((HALF, SLOTS), BF),
        pltpu.VMEM((NODES, EDGES), BF),
        pltpu.VMEM((HALF, D), F32),
        pltpu.VMEM((SLOTS, D), BF),
        pltpu.VMEM((NODES, D), F32),
        pltpu.VMEM((NODES, D), F32),
        pltpu.VMEM((NODES, D), BF),
        pltpu.VMEM((EDGES, 1), F32),
        pltpu.VMEM((2, D, D), BF),
        pltpu.VMEM((2, 2, D, D), BF),
        pltpu.VMEM((2, D, D), BF),
        pltpu.VMEM((2, 4, D), F32),
        pltpu.VMEM((2, 2, D), F32),
        pltpu.VMEM((2, 2, D), F32),
    )
    passed = pl.pallas_call(
        kernel,
        out_shape=held,
        in_specs=[hbm] * 13,
        out_specs=(vmem,) * len(held),
        scratch_shapes=[
            pltpu.VMEM((2, D + 2 * NODES, D), BF),
            pltpu.VMEM((2, D, D), BF),
            pltpu.VMEM((2, D, D), BF),
            pltpu.VMEM((SLOTS, NODES), BF),
            pltpu.VMEM((PEERS, 16, 128), BF),
            pltpu.VMEM((2, PEERS, 16, 128), BF),
            pltpu.VMEM((16, 16, 128), BF),
            pltpu.VMEM((16, 128), jnp.int32),
            pltpu.VMEM((16, 128), jnp.int32),
            pltpu.VMEM((16, 128), jnp.int32),
            pltpu.VMEM((CAP, PEERS), jnp.int32),
            pltpu.SemaphoreType.DMA((2,)),
            pltpu.SemaphoreType.DMA((2, 2)),
            pltpu.SemaphoreType.DMA((3,)),
            pltpu.SemaphoreType.REGULAR,
            pltpu.SemaphoreType.DMA((22,)),
        ],
        compiler_params=pltpu.CompilerParams(
            collective_id=0, has_side_effects=True, vmem_limit_bytes=28 * 2**20
        ),
    )(*[pltpu.with_memory_space_constraint(a, pltpu.HBM) for a in args])
    return pl.pallas_call(
        finish,
        out_shape=(pltpu.HBM((NODES, D), BF), pltpu.HBM((EDGES, D), BF)),
        in_specs=[vmem] * len(held),
        out_specs=(hbm, hbm),
        scratch_shapes=[
            pltpu.VMEM((HALF, D), BF),
            pltpu.VMEM((NODES, D), BF),
            pltpu.SemaphoreType.DMA((3,)),
        ],
        compiler_params=pltpu.CompilerParams(vmem_limit_bytes=20 * 2**20),
    )(*passed)


def solution(mesh):
    in_specs = (
        P(("dp", "dom"), None),
        P(("dp", "dom"), None),
        P(("dp", "dom")),
        P(("dp", "dom")),
        P(("dp", "dom")),
        P(("dp", "dom"), None, None),
        P(),
        P(),
        P(),
        P(),
        P(),
        P(),
        P(),
    )
    out_specs = (P(("dp", "dom"), None), P(("dp", "dom"), None))
    return jax.shard_map(local, mesh=mesh, in_specs=in_specs, out_specs=out_specs, check_vma=False)
```

```python
import jax
import jax.numpy as jnp
from jax import lax
from jax.experimental import pallas as pl
from jax.experimental.pallas import tpu as pltpu
from jax.sharding import PartitionSpec as P

MESH = pl.DeviceIdType.MESH
BF = jnp.bfloat16
F32 = jnp.float32

PEERS, CAP, NODES, EDGES, D = 128, 4, 256, 2048, 512
HALF = EDGES // 2
SLOTS = PEERS * CAP
NX, NZ, NY = 4, 8, 4
TILE = 1024
DZ_ORDER = (4, 3, 5, 2, 6, 1, 7)


def dot(a, b):
    return jnp.dot(a, b, preferred_element_type=F32)


def silu(v):
    half = 0.5 * v
    return half * jnp.tanh(half) + half


def layer_norm(values, gain, shift):
    mean = jnp.mean(values, axis=-1, keepdims=True)
    centered = values - mean
    variance = jnp.mean(centered * centered, axis=-1, keepdims=True)
    return centered * lax.rsqrt(variance + 1e-05) * gain + shift


def swap_pairs(even, odd):
    low = lax.broadcasted_iota(jnp.int32, (1, 8, 128), 1) < 4
    first = jnp.where(low, even, pltpu.roll(odd, 4, 1))
    second = jnp.where(low, pltpu.roll(even, 4, 1), odd)
    return first, second


def slot_of(dx, dz, dy):
    plane = dy * NX + dx
    rank = jnp.where(dz < 4, 7 - 2 * dz, 2 * dz - 8)
    off_plane = jnp.where(rank < 2, 16 + 16 * rank + plane, 54 + plane * 5 - rank)
    return jnp.where(dz == 0, plane, off_plane)


def edge_tail(hidden, state, live, w_out, bias, gain, shift):
    act = silu(hidden.astype(BF))
    projected = dot(act, w_out) + bias[1:2, :]
    message = layer_norm(projected, gain[0:1, :], shift[0:1, :])
    message = jnp.where(live > 0, message, 0.0).astype(BF)
    return message, state + message


def remote_edges(tr, halo, hpre, xr, mask_col, agg_t, agg_acc, state_ref, w_out, bias, gain, shift):
    total = agg_acc[...]
    for t in range(HALF // TILE):
        rows, later = pl.ds(t * TILE, TILE), pl.ds(HALF + t * TILE, TILE)
        hidden = dot(tr[rows, pl.ds(0, SLOTS // 2)], halo[pl.ds(0, SLOTS // 2), :]) + hpre[rows, :]
        message, state = edge_tail(
            hidden, xr[rows, pl.ds(0, D)], mask_col[later, :], w_out, bias, gain, shift
        )
        state_ref[rows, pl.ds(0, D)] = state
        total = total + dot(agg_t[:, later], message)
    return total.astype(BF)


def node_step(total, nh_pre, node_state, w_in, w_out, bias, gain, shift):
    act = silu(nh_pre[...] + dot(total, w_in)).astype(BF)
    projected = dot(act, w_out) + bias[3:4, :]
    update = layer_norm(projected, gain[1:2, :], shift[1:2, :])
    return (node_state[...].astype(F32) + update).astype(BF)


def kernel(
    node_hbm, edge_hbm, sender_hbm, receiver_hbm, mask_hbm, list_hbm,
    edge_in_hbm, edge_out_hbm, node_in_hbm, node_out_hbm, bias_hbm, gain_hbm, shift_hbm,
    xl, xr, tr, agg_t, hpre, halo, agg_acc, nh_pre, node_state, mask_col,
    w_out, n_in, n_out, bias_ref, gain_ref, shift_ref,
    wcat, w_send, w_recv, pick, sbuf, rbuf, bundled,
    sender_ref, receiver_ref, mask_ref, list_ref,
    ssem, rsem, bsem, ready, lsem,
):
    me = lax.axis_index("dom")
    x, z, y = lax.rem(me, NX), lax.rem(me // NX, NZ), me // (NX * NZ)

    def peer(dx, dz, dy):
        return (lax.rem(y + dy, NY) * NZ + lax.rem(z + dz, NZ)) * NX + lax.rem(x + dx, NX)

    def tell(sem, target):
        pl.semaphore_signal(sem, inc=1, device_id={"dom": target}, device_id_type=MESH)

    loads = {}

    def load(name, src, dst):
        copy = pltpu.make_async_copy(src, dst, lsem.at[len(loads)])
        copy.start()
        loads[name] = copy

    load("list", list_hbm, list_ref)
    load("node", node_hbm, node_state)
    load("send0", edge_in_hbm.at[0, 1], w_send.at[0])
    load("senders", sender_hbm, sender_ref)
    load("receivers", receiver_hbm, receiver_ref)
    load("masks", mask_hbm, mask_ref)

    barrier = pltpu.get_barrier_semaphore()
    for plane in range(1, NX * NY):
        tell(barrier, peer(plane % NX, 0, plane // NX))
    for dz in range(1, NZ):
        tell(barrier, peer(0, dz, 0))

    p = lax.broadcasted_iota(jnp.int32, (1, PEERS), 1)
    to = slot_of((p - x) & (NX - 1), ((p >> 2) - z) & (NZ - 1), ((p >> 5) - y) & (NY - 1))
    spread = (lax.broadcasted_iota(jnp.int32, (SLOTS, PEERS), 0) // CAP == to).astype(BF)
    loads["list"].wait()
    lists = lax.dot_general(
        spread, list_ref[...].astype(F32).astype(BF), (((1,), (1,)), ((), ())), preferred_element_type=F32
    )
    own = lax.broadcasted_iota(jnp.int32, (SLOTS, CAP), 0) % CAP == lax.broadcasted_iota(
        jnp.int32, (SLOTS, CAP), 1
    )
    chosen = jnp.sum(jnp.where(own, lists, 0.0), axis=1, keepdims=True).astype(jnp.int32)
    pick[...] = (chosen == lax.broadcasted_iota(jnp.int32, (SLOTS, NODES), 1)).astype(BF)
    for r in range(2):
        rbuf[r, 0] = jnp.zeros((16, 128), BF)

    def project_and_pack(r):
        loads[f"send{r}"].wait()
        send_proj = dot(node_state[...], w_send[r]).astype(BF)
        wcat[r, pl.ds(D + NODES, NODES), :] = send_proj
        rows = dot(pick[...], send_proj)
        for h in range(2):
            first, second = swap_pairs(
                rows[:, 256 * h : 256 * h + 128].reshape(PEERS // 2, 8, 128),
                rows[:, 256 * h + 128 : 256 * h + 256].reshape(PEERS // 2, 8, 128),
            )
            part = jnp.stack([first, second], axis=1).reshape(PEERS, 8, 128)
            if h == 0:
                upper = part
        sbuf[...] = jnp.concatenate([upper, part], axis=1).astype(BF)

    def send(r, group, slot, target):
        pltpu.make_async_remote_copy(
            src_ref=sbuf.at[slot],
            dst_ref=rbuf.at[r, slot],
            send_sem=ssem.at[r],
            recv_sem=rsem.at[r, group],
            device_id={"dom": target},
            device_id_type=MESH,
        ).start()

    def send_off_plane(r, group, plane, ranks):
        for rank in ranks:
            slot = 16 + 16 * rank + plane if rank < 2 else 54 + plane * 5 - rank
            send(
                r, 1 if rank < 2 else group, slot,
                peer(lax.rem(plane, NX), DZ_ORDER[rank], plane // NX),
            )

    def send_far(r):
        start = 2 * (r == 0)

        def first(j, carry):
            send_off_plane(r, 0, 15 - j, range(start, 7))
            return carry

        def second(j, carry):
            send_off_plane(r, 1, 2 - j, range(start, 7))
            return carry

        lax.fori_loop(0, 12, first, 0)
        send_off_plane(r, 0, 3, range(start, 6))
        send_off_plane(r, 1, 3, range(6, 7))
        lax.fori_loop(0, 2, second, 0)

    def send_line(r):
        send_off_plane(r, 1, 0, range(2 * (r == 0), 7))

    def bundle(k):
        return pltpu.make_async_remote_copy(
            src_ref=sbuf.at[pl.ds(16 + 16 * k, 16)],
            dst_ref=bundled.at[k],
            send_sem=bsem.at[0, k],
            recv_sem=bsem.at[1, k],
            device_id={"dom": peer(0, DZ_ORDER[k], 0)},
            device_id_type=MESH,
        )

    def forward_bundle(k):
        bundle(k).wait()

        def body(plane, carry):
            pltpu.make_async_remote_copy(
                src_ref=bundled.at[k, plane],
                dst_ref=rbuf.at[0, 16 + 16 * k + plane],
                send_sem=bsem.at[2, k],
                recv_sem=rsem.at[0, 1],
                device_id={"dom": peer(lax.rem(plane, NX), 0, plane // NX)},
                device_id_type=MESH,
            ).start()
            return carry

        lax.fori_loop(1, NX * NY, body, 0)
        rbuf[0, 16 + 16 * k] = bundled[k, 0]

    def send_plane(r):
        def body(plane, carry):
            send(r, 1, plane, peer(lax.rem(plane, NX), 0, plane // NX))
            return carry

        lax.fori_loop(1, NX * NY, body, 0)

    def arrived(r, first, count, group):
        return pltpu.make_async_remote_copy(
            src_ref=sbuf.at[pl.ds(first, count)],
            dst_ref=rbuf.at[r, pl.ds(first, count)],
            send_sem=ssem.at[r],
            recv_sem=rsem.at[r, group],
            device_id={"dom": lax.rem(me + 1, PEERS)},
            device_id_type=MESH,
        )

    def receive(r, group):
        if group == 0:
            arrived(r, 64, 64, 0).wait_recv()
        else:
            arrived(r, 1, 63 - 2 * (r == 0), 1).wait_recv()
        first, rows = (1 - group) * 64, SLOTS // 2
        got = rbuf[r, pl.ds(first, 64)].astype(F32).reshape(32, 2, 2, 8, 128)
        for h in range(2):
            left, right = swap_pairs(got[:, 0, h], got[:, 1, h])
            at = pl.ds(first * CAP, rows)
            halo[at, 256 * h : 256 * h + 128] = left.reshape(rows, 128).astype(BF)
            halo[at, 256 * h + 128 : 256 * h + 256] = right.reshape(rows, 128).astype(BF)

    def remote_half(r):
        for t in range(HALF // TILE):
            rows, late = pl.ds(t * TILE, TILE), pl.ds(SLOTS // 2, SLOTS // 2)
            hpre[rows, :] = hpre[rows, :] + dot(tr[rows, late], halo[late, :])

    def tables():
        far = sender_ref[...] - NODES
        at = slot_of(
            (x - (far >> 2)) & (NX - 1), (z - (far >> 4)) & (NZ - 1), (y - (far >> 7)) & (NY - 1)
        )
        senders = jnp.transpose(jnp.where(far >= 0, at * CAP + (far & (CAP - 1)), sender_ref[...]))
        receivers = jnp.transpose(receiver_ref[...])
        masks = jnp.transpose(mask_ref[...])
        nodes = lax.broadcasted_iota(jnp.int32, (128, NODES), 1)
        slots = lax.broadcasted_iota(jnp.int32, (128, SLOTS), 1)
        node_rows = lax.broadcasted_iota(jnp.int32, (NODES, 128), 0)
        for j in range(EDGES // 128):
            rows = pl.ds(j % 8 * 128, 128)
            mask_col[pl.ds(j * 128, 128), :] = masks[:, j : j + 1].astype(F32)
            received = (receivers[:, j : j + 1] == nodes).astype(BF)
            if j < 8:
                xl[rows, pl.ds(D, NODES)] = received
                xl[rows, pl.ds(D + NODES, NODES)] = (senders[:, j : j + 1] == nodes).astype(BF)
            else:
                xr[rows, pl.ds(D, NODES)] = received
                tr[rows, :] = (senders[:, j : j + 1] == slots).astype(BF)
            live = jnp.where(mask_ref[j : j + 1, :] > 0, receiver_ref[j : j + 1, :], -1)
            agg_t[:, pl.ds(j * 128, 128)] = (live == node_rows).astype(BF)

    def local_edges(r):
        total = jnp.zeros((NODES, D), F32)
        for t in range(HALF // TILE):
            rows = pl.ds(t * TILE, TILE)
            hidden = dot(xl[rows, :], wcat[r]) + bias_ref[r, 0:1, :]
            message, state = edge_tail(
                hidden, xl[rows, pl.ds(0, D)], mask_col[rows, :],
                w_out[r], bias_ref[r], gain_ref[r], shift_ref[r],
            )
            xl[rows, pl.ds(0, D)] = state
            total = total + dot(agg_t[:, rows], message)
        agg_acc[...] = total

    def remote_start(r):
        for t in range(HALF // TILE):
            rows = pl.ds(t * TILE, TILE)
            hpre[rows, :] = dot(xr[rows, :], wcat[r, pl.ds(0, D + NODES), :]) + bias_ref[r, 0:1, :]

    loads["node"].wait()
    project_and_pack(0)
    pl.semaphore_wait(barrier, NZ - 1 + NX * NY - 1)
    for dz in range(1, NZ):
        tell(ready, peer(0, dz, 0))
    for k in range(2):
        bundle(k).start()
    send_line(0)
    load("biases", bias_hbm, bias_ref)
    load("gains", gain_hbm, gain_ref)
    load("shifts", shift_hbm, shift_ref)
    load("recv0", edge_in_hbm.at[0, 2], w_recv.at[0])
    load("edge0", edge_in_hbm.at[0, 0], wcat.at[0, pl.ds(0, D)])
    load("xl", edge_hbm.at[pl.ds(0, HALF)], xl.at[:, pl.ds(0, D)])
    load("out0", edge_out_hbm.at[0], w_out.at[0])
    load("xr", edge_hbm.at[pl.ds(HALF, HALF)], xr.at[:, pl.ds(0, D)])
    load("nin0", node_in_hbm.at[0], n_in.at[0])
    load("nout0", node_out_hbm.at[0], n_out.at[0])
    load("send1", edge_in_hbm.at[1, 1], w_send.at[1])
    load("recv1", edge_in_hbm.at[1, 2], w_recv.at[1])
    load("edge1", edge_in_hbm.at[1, 0], wcat.at[1, pl.ds(0, D)])
    load("out1", edge_out_hbm.at[1], w_out.at[1])
    load("nin1", node_in_hbm.at[1], n_in.at[1])
    load("nout1", node_out_hbm.at[1], n_out.at[1])
    for name in ("senders", "receivers", "masks"):
        loads[name].wait()
    tables()
    pl.semaphore_wait(ready, NZ - 1)
    send_far(0)
    for k in range(2):
        forward_bundle(k)
    send_plane(0)
    for name in ("biases", "gains", "shifts"):
        loads[name].wait()

    for r in range(2):
        loads[f"recv{r}"].wait()
        wcat[r, pl.ds(D, NODES), :] = dot(node_state[...], w_recv[r]).astype(BF)
        if r == 0:
            loads["xl"].wait()
            loads["xr"].wait()
        loads[f"edge{r}"].wait()
        loads[f"out{r}"].wait()
        local_edges(r)
        remote_start(r)
        loads[f"nin{r}"].wait()
        loads[f"nout{r}"].wait()
        nh_pre[...] = dot(node_state[...], n_in[r, 0]) + bias_ref[r, 2:3, :]
        receive(r, 0)
        remote_half(r)
        arrived(r, 0, 95 if r == 0 else 127, 0).wait_send()
        if r == 0:
            for k in range(2):
                pltpu.make_async_remote_copy(
                    src_ref=bundled.at[k, pl.ds(1, 15)],
                    dst_ref=rbuf.at[0, pl.ds(1, 15)],
                    send_sem=bsem.at[2, k],
                    recv_sem=rsem.at[0, 1],
                    device_id={"dom": lax.rem(me + 1, PEERS)},
                    device_id_type=MESH,
                ).wait_send()
        receive(r, 1)
        if r == 0:
            total = remote_edges(
                tr, halo, hpre, xr, mask_col, agg_t, agg_acc, xr,
                w_out[r], bias_ref[r], gain_ref[r], shift_ref[r],
            )
            node_state[...] = node_step(
                total, nh_pre, node_state,
                n_in[r, 1], n_out[r], bias_ref[r], gain_ref[r], shift_ref[r],
            )
            project_and_pack(1)
            send_far(1)
            send_line(1)
            send_plane(1)


def finish(
    xl, xr, tr, agg_t, hpre, halo, agg_acc, nh_pre, node_state, mask_col,
    w_out, n_in, n_out, bias_ref, gain_ref, shift_ref,
    node_out_hbm, edge_out_hbm,
    state, node_new, osem,
):
    near = pltpu.make_async_copy(xl.at[:, pl.ds(0, D)], edge_out_hbm.at[pl.ds(0, HALF)], osem.at[0])
    near.start()
    total = remote_edges(
        tr, halo, hpre, xr, mask_col, agg_t, agg_acc, state,
        w_out[1], bias_ref[1], gain_ref[1], shift_ref[1],
    )
    far = pltpu.make_async_copy(state, edge_out_hbm.at[pl.ds(HALF, HALF)], osem.at[1])
    far.start()
    node_new[...] = node_step(
        total, nh_pre, node_state,
        n_in[1, 1], n_out[1], bias_ref[1], gain_ref[1], shift_ref[1],
    )
    nodes = pltpu.make_async_copy(node_new, node_out_hbm, osem.at[2])
    nodes.start()
    near.wait()
    far.wait()
    nodes.wait()


def local(
    node_latent, edge_latent, edge_sender, edge_receiver, edge_mask, send_list,
    edge_in, edge_out, node_in, node_out, biases, ln_gain, ln_shift,
):
    hbm = pl.BlockSpec(memory_space=pltpu.HBM)
    vmem = pl.BlockSpec(memory_space=pltpu.VMEM)
    args = [
        node_latent, edge_latent,
        edge_sender.reshape(16, 128), edge_receiver.reshape(16, 128), edge_mask.reshape(16, 128),
        send_list.reshape(PEERS, CAP).T,
        edge_in, edge_out, node_in, node_out, biases, ln_gain, ln_shift,
    ]
    held = (
        pltpu.VMEM((HALF, D + 2 * NODES), BF),
        pltpu.VMEM((HALF, D + NODES), BF),
        pltpu.VMEM((HALF, SLOTS), BF),
        pltpu.VMEM((NODES, EDGES), BF),
        pltpu.VMEM((HALF, D), F32),
        pltpu.VMEM((SLOTS, D), BF),
        pltpu.VMEM((NODES, D), F32),
        pltpu.VMEM((NODES, D), F32),
        pltpu.VMEM((NODES, D), BF),
        pltpu.VMEM((EDGES, 1), F32),
        pltpu.VMEM((2, D, D), BF),
        pltpu.VMEM((2, 2, D, D), BF),
        pltpu.VMEM((2, D, D), BF),
        pltpu.VMEM((2, 4, D), F32),
        pltpu.VMEM((2, 2, D), F32),
        pltpu.VMEM((2, 2, D), F32),
    )
    passed = pl.pallas_call(
        kernel,
        out_shape=held,
        in_specs=[hbm] * 13,
        out_specs=(vmem,) * len(held),
        scratch_shapes=[
            pltpu.VMEM((2, D + 2 * NODES, D), BF),
            pltpu.VMEM((2, D, D), BF),
            pltpu.VMEM((2, D, D), BF),
            pltpu.VMEM((SLOTS, NODES), BF),
            pltpu.VMEM((PEERS, 16, 128), BF),
            pltpu.VMEM((2, PEERS, 16, 128), BF),
            pltpu.VMEM((2, 16, 16, 128), BF),
            pltpu.VMEM((16, 128), jnp.int32),
            pltpu.VMEM((16, 128), jnp.int32),
            pltpu.VMEM((16, 128), jnp.int32),
            pltpu.VMEM((CAP, PEERS), jnp.int32),
            pltpu.SemaphoreType.DMA((2,)),
            pltpu.SemaphoreType.DMA((2, 2)),
            pltpu.SemaphoreType.DMA((3, 2)),
            pltpu.SemaphoreType.REGULAR,
            pltpu.SemaphoreType.DMA((22,)),
        ],
        compiler_params=pltpu.CompilerParams(
            collective_id=0, has_side_effects=True, vmem_limit_bytes=28 * 2**20
        ),
    )(*[pltpu.with_memory_space_constraint(a, pltpu.HBM) for a in args])
    return pl.pallas_call(
        finish,
        out_shape=(pltpu.HBM((NODES, D), BF), pltpu.HBM((EDGES, D), BF)),
        in_specs=[vmem] * len(held),
        out_specs=(hbm, hbm),
        scratch_shapes=[
            pltpu.VMEM((HALF, D), BF),
            pltpu.VMEM((NODES, D), BF),
            pltpu.SemaphoreType.DMA((3,)),
        ],
        compiler_params=pltpu.CompilerParams(vmem_limit_bytes=20 * 2**20),
    )(*passed)


def solution(mesh):
    in_specs = (
        P(("dp", "dom"), None),
        P(("dp", "dom"), None),
        P(("dp", "dom")),
        P(("dp", "dom")),
        P(("dp", "dom")),
        P(("dp", "dom"), None, None),
        P(),
        P(),
        P(),
        P(),
        P(),
        P(),
        P(),
    )
    out_specs = (P(("dp", "dom"), None), P(("dp", "dom"), None))
    return jax.shard_map(local, mesh=mesh, in_specs=in_specs, out_specs=out_specs, check_vma=False)
```

```python
import jax
import jax.numpy as jnp
from jax import lax
from jax.experimental import pallas as pl
from jax.experimental.pallas import tpu as pltpu
from jax.sharding import PartitionSpec as P

MESH = pl.DeviceIdType.MESH
BF = jnp.bfloat16
F32 = jnp.float32

PEERS, CAP, NODES, EDGES, D = 128, 4, 256, 2048, 512
HALF = EDGES // 2
SLOTS = PEERS * CAP
NX, NZ, NY = 4, 8, 4
TILE = 1024
DZ_ORDER = (4, 3, 5, 2, 6, 1, 7)


def dot(a, b):
    return jnp.dot(a, b, preferred_element_type=F32)


def silu(v):
    half = 0.5 * v
    return half * jnp.tanh(half) + half


def layer_norm(values, gain, shift):
    mean = jnp.mean(values, axis=-1, keepdims=True)
    centered = values - mean
    variance = jnp.mean(centered * centered, axis=-1, keepdims=True)
    return centered * lax.rsqrt(variance + 1e-05) * gain + shift


def swap_pairs(even, odd):
    low = lax.broadcasted_iota(jnp.int32, (1, 8, 128), 1) < 4
    first = jnp.where(low, even, pltpu.roll(odd, 4, 1))
    second = jnp.where(low, pltpu.roll(even, 4, 1), odd)
    return first, second


def slot_of(dx, dz, dy):
    plane = dy * NX + dx
    rank = jnp.where(dz < 4, 7 - 2 * dz, 2 * dz - 8)
    near = jnp.where(dz == 0, plane, 16 + plane)
    return jnp.where((dz == 0) | (dz == 4), near, 38 + plane * 6 - rank)


def edge_tail(hidden, state, live, w_out, bias, gain, shift):
    act = silu(hidden.astype(BF))
    projected = dot(act, w_out) + bias[1:2, :]
    message = layer_norm(projected, gain[0:1, :], shift[0:1, :])
    message = jnp.where(live > 0, message, 0.0).astype(BF)
    return message, state + message


def remote_edges(tr, halo, hpre, xr, mask_col, agg_t, agg_acc, state_ref, w_out, bias, gain, shift):
    total = agg_acc[...]
    for t in range(HALF // TILE):
        rows, later = pl.ds(t * TILE, TILE), pl.ds(HALF + t * TILE, TILE)
        hidden = dot(tr[rows, pl.ds(0, SLOTS // 2)], halo[pl.ds(0, SLOTS // 2), :]) + hpre[rows, :]
        message, state = edge_tail(
            hidden, xr[rows, pl.ds(0, D)], mask_col[later, :], w_out, bias, gain, shift
        )
        state_ref[rows, pl.ds(0, D)] = state
        total = total + dot(agg_t[:, later], message)
    return total.astype(BF)


def node_step(total, nh_pre, node_state, w_in, w_out, bias, gain, shift):
    act = silu(nh_pre[...] + dot(total, w_in)).astype(BF)
    projected = dot(act, w_out) + bias[3:4, :]
    update = layer_norm(projected, gain[1:2, :], shift[1:2, :])
    return (node_state[...].astype(F32) + update).astype(BF)


def kernel(
    node_hbm, edge_hbm, sender_hbm, receiver_hbm, mask_hbm, list_hbm,
    edge_in_hbm, edge_out_hbm, node_in_hbm, node_out_hbm, bias_hbm, gain_hbm, shift_hbm,
    xl, xr, tr, agg_t, hpre, halo, agg_acc, nh_pre, node_state, mask_col,
    w_out, n_in, n_out, bias_ref, gain_ref, shift_ref,
    wcat, w_send, w_recv, pick, sbuf, rbuf, bundled,
    sender_ref, receiver_ref, mask_ref, list_ref,
    ssem, rsem, bsem, ready, lsem,
):
    me = lax.axis_index("dom")
    x, z, y = lax.rem(me, NX), lax.rem(me // NX, NZ), me // (NX * NZ)

    def peer(dx, dz, dy):
        return (lax.rem(y + dy, NY) * NZ + lax.rem(z + dz, NZ)) * NX + lax.rem(x + dx, NX)

    def tell(sem, target):
        pl.semaphore_signal(sem, inc=1, device_id={"dom": target}, device_id_type=MESH)

    loads = {}

    def load(name, src, dst):
        copy = pltpu.make_async_copy(src, dst, lsem.at[len(loads)])
        copy.start()
        loads[name] = copy

    load("list", list_hbm, list_ref)
    load("node", node_hbm, node_state)
    load("send0", edge_in_hbm.at[0, 1], w_send.at[0])

    barrier = pltpu.get_barrier_semaphore()
    for plane in range(1, NX * NY):
        tell(barrier, peer(plane % NX, 0, plane // NX))
    for dz in range(1, NZ):
        tell(barrier, peer(0, dz, 0))

    p = lax.broadcasted_iota(jnp.int32, (1, PEERS), 1)
    to = slot_of((p - x) & (NX - 1), ((p >> 2) - z) & (NZ - 1), ((p >> 5) - y) & (NY - 1))
    spread = (lax.broadcasted_iota(jnp.int32, (SLOTS, PEERS), 0) // CAP == to).astype(BF)
    loads["list"].wait()
    lists = lax.dot_general(
        spread, list_ref[...].astype(F32).astype(BF), (((1,), (1,)), ((), ())), preferred_element_type=F32
    )
    own = lax.broadcasted_iota(jnp.int32, (SLOTS, CAP), 0) % CAP == lax.broadcasted_iota(
        jnp.int32, (SLOTS, CAP), 1
    )
    chosen = jnp.sum(jnp.where(own, lists, 0.0), axis=1, keepdims=True).astype(jnp.int32)
    pick[...] = (chosen == lax.broadcasted_iota(jnp.int32, (SLOTS, NODES), 1)).astype(BF)
    for r in range(2):
        rbuf[r, 0] = jnp.zeros((16, 128), BF)

    def project_and_pack(r):
        loads[f"send{r}"].wait()
        send_proj = dot(node_state[...], w_send[r]).astype(BF)
        wcat[r, pl.ds(D + NODES, NODES), :] = send_proj
        rows = dot(pick[...], send_proj)
        for h in range(2):
            first, second = swap_pairs(
                rows[:, 256 * h : 256 * h + 128].reshape(PEERS // 2, 8, 128),
                rows[:, 256 * h + 128 : 256 * h + 256].reshape(PEERS // 2, 8, 128),
            )
            part = jnp.stack([first, second], axis=1).reshape(PEERS, 8, 128)
            if h == 0:
                upper = part
        sbuf[...] = jnp.concatenate([upper, part], axis=1).astype(BF)

    def send(r, group, slot, target):
        pltpu.make_async_remote_copy(
            src_ref=sbuf.at[slot],
            dst_ref=rbuf.at[r, slot],
            send_sem=ssem.at[r],
            recv_sem=rsem.at[r, group],
            device_id={"dom": target},
            device_id_type=MESH,
        ).start()

    def send_off_plane(r, group, plane, ranks, opposite):
        if opposite:
            send(r, 1, 16 + plane, peer(lax.rem(plane, NX), 4, plane // NX))
        for rank in ranks:
            send(r, group, 38 + plane * 6 - rank, peer(lax.rem(plane, NX), DZ_ORDER[rank], plane // NX))

    def send_far(r):
        def first(j, carry):
            send_off_plane(r, 0, 15 - j, range(1, 7), r == 1)
            return carry

        def second(j, carry):
            send_off_plane(r, 1, 4 - j, range(1, 7), r == 1)
            return carry

        lax.fori_loop(0, 10, first, 0)
        send_off_plane(r, 0, 5, range(1, 5), r == 1)
        send_off_plane(r, 1, 5, range(5, 7), False)
        lax.fori_loop(0, 4, second, 0)

    def send_line(r):
        send_off_plane(r, 1, 0, range(1, 7), r == 1)

    def bundle():
        return pltpu.make_async_remote_copy(
            src_ref=sbuf.at[pl.ds(16, 16)],
            dst_ref=bundled,
            send_sem=bsem.at[0],
            recv_sem=bsem.at[1],
            device_id={"dom": peer(0, 4, 0)},
            device_id_type=MESH,
        )

    def forward(plane):
        return pltpu.make_async_remote_copy(
            src_ref=bundled.at[plane],
            dst_ref=rbuf.at[0, 16 + plane],
            send_sem=bsem.at[2],
            recv_sem=rsem.at[0, 1],
            device_id={"dom": peer(lax.rem(plane, NX), 0, plane // NX)},
            device_id_type=MESH,
        )

    def forward_bundle():
        bundle().wait()

        def body(plane, carry):
            forward(plane).start()
            return carry

        lax.fori_loop(1, NX * NY, body, 0)
        rbuf[0, 16] = bundled[0]

    def send_plane(r):
        def body(plane, carry):
            send(r, 1, plane, peer(lax.rem(plane, NX), 0, plane // NX))
            return carry

        lax.fori_loop(1, NX * NY, body, 0)

    def arrived(r, first, count, group):
        return pltpu.make_async_remote_copy(
            src_ref=sbuf.at[pl.ds(first, count)],
            dst_ref=rbuf.at[r, pl.ds(first, count)],
            send_sem=ssem.at[r],
            recv_sem=rsem.at[r, group],
            device_id={"dom": lax.rem(me + 1, PEERS)},
            device_id_type=MESH,
        )

    def receive(r, group):
        if group == 0:
            arrived(r, 64, 64, 0).wait_recv()
        else:
            arrived(r, 1, 63 - (r == 0), 1).wait_recv()
        first, rows = (1 - group) * 64, SLOTS // 2
        got = rbuf[r, pl.ds(first, 64)].astype(F32).reshape(32, 2, 2, 8, 128)
        for h in range(2):
            left, right = swap_pairs(got[:, 0, h], got[:, 1, h])
            at = pl.ds(first * CAP, rows)
            halo[at, 256 * h : 256 * h + 128] = left.reshape(rows, 128).astype(BF)
            halo[at, 256 * h + 128 : 256 * h + 256] = right.reshape(rows, 128).astype(BF)

    def remote_half(r):
        for t in range(HALF // TILE):
            rows, late = pl.ds(t * TILE, TILE), pl.ds(SLOTS // 2, SLOTS // 2)
            hpre[rows, :] = hpre[rows, :] + dot(tr[rows, late], halo[late, :])

    def tables():
        far = sender_ref[...] - NODES
        at = slot_of(
            (x - (far >> 2)) & (NX - 1), (z - (far >> 4)) & (NZ - 1), (y - (far >> 7)) & (NY - 1)
        )
        senders = jnp.transpose(jnp.where(far >= 0, at * CAP + (far & (CAP - 1)), sender_ref[...]))
        receivers = jnp.transpose(receiver_ref[...])
        masks = jnp.transpose(mask_ref[...])
        nodes = lax.broadcasted_iota(jnp.int32, (128, NODES), 1)
        slots = lax.broadcasted_iota(jnp.int32, (128, SLOTS), 1)
        node_rows = lax.broadcasted_iota(jnp.int32, (NODES, 128), 0)
        for j in range(EDGES // 128):
            rows = pl.ds(j % 8 * 128, 128)
            mask_col[pl.ds(j * 128, 128), :] = masks[:, j : j + 1].astype(F32)
            received = (receivers[:, j : j + 1] == nodes).astype(BF)
            if j < 8:
                xl[rows, pl.ds(D, NODES)] = received
                xl[rows, pl.ds(D + NODES, NODES)] = (senders[:, j : j + 1] == nodes).astype(BF)
            else:
                xr[rows, pl.ds(D, NODES)] = received
                tr[rows, :] = (senders[:, j : j + 1] == slots).astype(BF)
            live = jnp.where(mask_ref[j : j + 1, :] > 0, receiver_ref[j : j + 1, :], -1)
            agg_t[:, pl.ds(j * 128, 128)] = (live == node_rows).astype(BF)

    def local_edges(r):
        total = jnp.zeros((NODES, D), F32)
        for t in range(HALF // TILE):
            rows = pl.ds(t * TILE, TILE)
            hidden = dot(xl[rows, :], wcat[r]) + bias_ref[r, 0:1, :]
            message, state = edge_tail(
                hidden, xl[rows, pl.ds(0, D)], mask_col[rows, :],
                w_out[r], bias_ref[r], gain_ref[r], shift_ref[r],
            )
            xl[rows, pl.ds(0, D)] = state
            total = total + dot(agg_t[:, rows], message)
        agg_acc[...] = total

    def remote_start(r):
        for t in range(HALF // TILE):
            rows = pl.ds(t * TILE, TILE)
            hpre[rows, :] = dot(xr[rows, :], wcat[r, pl.ds(0, D + NODES), :]) + bias_ref[r, 0:1, :]

    loads["node"].wait()
    project_and_pack(0)
    pl.semaphore_wait(barrier, NZ - 1 + NX * NY - 1)
    for dz in range(1, NZ):
        tell(ready, peer(0, dz, 0))
    bundle().start()
    send_line(0)
    load("senders", sender_hbm, sender_ref)
    load("receivers", receiver_hbm, receiver_ref)
    load("masks", mask_hbm, mask_ref)
    load("biases", bias_hbm, bias_ref)
    load("gains", gain_hbm, gain_ref)
    load("shifts", shift_hbm, shift_ref)
    load("recv0", edge_in_hbm.at[0, 2], w_recv.at[0])
    load("edge0", edge_in_hbm.at[0, 0], wcat.at[0, pl.ds(0, D)])
    load("xl", edge_hbm.at[pl.ds(0, HALF)], xl.at[:, pl.ds(0, D)])
    load("out0", edge_out_hbm.at[0], w_out.at[0])
    load("xr", edge_hbm.at[pl.ds(HALF, HALF)], xr.at[:, pl.ds(0, D)])
    load("nin0", node_in_hbm.at[0], n_in.at[0])
    load("nout0", node_out_hbm.at[0], n_out.at[0])
    load("send1", edge_in_hbm.at[1, 1], w_send.at[1])
    load("recv1", edge_in_hbm.at[1, 2], w_recv.at[1])
    load("edge1", edge_in_hbm.at[1, 0], wcat.at[1, pl.ds(0, D)])
    load("out1", edge_out_hbm.at[1], w_out.at[1])
    load("nin1", node_in_hbm.at[1], n_in.at[1])
    load("nout1", node_out_hbm.at[1], n_out.at[1])
    pl.semaphore_wait(ready, NZ - 1)
    send_far(0)
    forward_bundle()
    send_plane(0)
    for name in ("senders", "receivers", "masks", "biases", "gains", "shifts"):
        loads[name].wait()
    tables()

    for r in range(2):
        loads[f"recv{r}"].wait()
        wcat[r, pl.ds(D, NODES), :] = dot(node_state[...], w_recv[r]).astype(BF)
        if r == 0:
            loads["xl"].wait()
            loads["xr"].wait()
        loads[f"edge{r}"].wait()
        loads[f"out{r}"].wait()
        local_edges(r)
        remote_start(r)
        loads[f"nin{r}"].wait()
        loads[f"nout{r}"].wait()
        nh_pre[...] = dot(node_state[...], n_in[r, 0]) + bias_ref[r, 2:3, :]
        receive(r, 0)
        remote_half(r)
        arrived(r, 0, 111 if r == 0 else 127, 0).wait_send()
        if r == 0:
            pltpu.make_async_remote_copy(
                src_ref=bundled.at[pl.ds(1, 15)],
                dst_ref=rbuf.at[0, pl.ds(1, 15)],
                send_sem=bsem.at[2],
                recv_sem=rsem.at[0, 1],
                device_id={"dom": lax.rem(me + 1, PEERS)},
                device_id_type=MESH,
            ).wait_send()
        receive(r, 1)
        if r == 0:
            total = remote_edges(
                tr, halo, hpre, xr, mask_col, agg_t, agg_acc, xr,
                w_out[r], bias_ref[r], gain_ref[r], shift_ref[r],
            )
            node_state[...] = node_step(
                total, nh_pre, node_state,
                n_in[r, 1], n_out[r], bias_ref[r], gain_ref[r], shift_ref[r],
            )
            project_and_pack(1)
            send_far(1)
            send_line(1)
            send_plane(1)


def finish(
    xl, xr, tr, agg_t, hpre, halo, agg_acc, nh_pre, node_state, mask_col,
    w_out, n_in, n_out, bias_ref, gain_ref, shift_ref,
    node_out_hbm, edge_out_hbm,
    state, node_new, osem,
):
    near = pltpu.make_async_copy(xl.at[:, pl.ds(0, D)], edge_out_hbm.at[pl.ds(0, HALF)], osem.at[0])
    near.start()
    total = remote_edges(
        tr, halo, hpre, xr, mask_col, agg_t, agg_acc, state,
        w_out[1], bias_ref[1], gain_ref[1], shift_ref[1],
    )
    far = pltpu.make_async_copy(state, edge_out_hbm.at[pl.ds(HALF, HALF)], osem.at[1])
    far.start()
    node_new[...] = node_step(
        total, nh_pre, node_state,
        n_in[1, 1], n_out[1], bias_ref[1], gain_ref[1], shift_ref[1],
    )
    nodes = pltpu.make_async_copy(node_new, node_out_hbm, osem.at[2])
    nodes.start()
    near.wait()
    far.wait()
    nodes.wait()


def local(
    node_latent, edge_latent, edge_sender, edge_receiver, edge_mask, send_list,
    edge_in, edge_out, node_in, node_out, biases, ln_gain, ln_shift,
):
    hbm = pl.BlockSpec(memory_space=pltpu.HBM)
    vmem = pl.BlockSpec(memory_space=pltpu.VMEM)
    args = [
        node_latent, edge_latent,
        edge_sender.reshape(16, 128), edge_receiver.reshape(16, 128), edge_mask.reshape(16, 128),
        send_list.reshape(PEERS, CAP).T,
        edge_in, edge_out, node_in, node_out, biases, ln_gain, ln_shift,
    ]
    held = (
        pltpu.VMEM((HALF, D + 2 * NODES), BF),
        pltpu.VMEM((HALF, D + NODES), BF),
        pltpu.VMEM((HALF, SLOTS), BF),
        pltpu.VMEM((NODES, EDGES), BF),
        pltpu.VMEM((HALF, D), F32),
        pltpu.VMEM((SLOTS, D), BF),
        pltpu.VMEM((NODES, D), F32),
        pltpu.VMEM((NODES, D), F32),
        pltpu.VMEM((NODES, D), BF),
        pltpu.VMEM((EDGES, 1), F32),
        pltpu.VMEM((2, D, D), BF),
        pltpu.VMEM((2, 2, D, D), BF),
        pltpu.VMEM((2, D, D), BF),
        pltpu.VMEM((2, 4, D), F32),
        pltpu.VMEM((2, 2, D), F32),
        pltpu.VMEM((2, 2, D), F32),
    )
    passed = pl.pallas_call(
        kernel,
        out_shape=held,
        in_specs=[hbm] * 13,
        out_specs=(vmem,) * len(held),
        scratch_shapes=[
            pltpu.VMEM((2, D + 2 * NODES, D), BF),
            pltpu.VMEM((2, D, D), BF),
            pltpu.VMEM((2, D, D), BF),
            pltpu.VMEM((SLOTS, NODES), BF),
            pltpu.VMEM((PEERS, 16, 128), BF),
            pltpu.VMEM((2, PEERS, 16, 128), BF),
            pltpu.VMEM((16, 16, 128), BF),
            pltpu.VMEM((16, 128), jnp.int32),
            pltpu.VMEM((16, 128), jnp.int32),
            pltpu.VMEM((16, 128), jnp.int32),
            pltpu.VMEM((CAP, PEERS), jnp.int32),
            pltpu.SemaphoreType.DMA((2,)),
            pltpu.SemaphoreType.DMA((2, 2)),
            pltpu.SemaphoreType.DMA((3,)),
            pltpu.SemaphoreType.REGULAR,
            pltpu.SemaphoreType.DMA((22,)),
        ],
        compiler_params=pltpu.CompilerParams(
            collective_id=0, has_side_effects=True, vmem_limit_bytes=28 * 2**20
        ),
    )(*[pltpu.with_memory_space_constraint(a, pltpu.HBM) for a in args])
    return pl.pallas_call(
        finish,
        out_shape=(pltpu.HBM((NODES, D), BF), pltpu.HBM((EDGES, D), BF)),
        in_specs=[vmem] * len(held),
        out_specs=(hbm, hbm),
        scratch_shapes=[
            pltpu.VMEM((HALF, D), BF),
            pltpu.VMEM((NODES, D), BF),
            pltpu.SemaphoreType.DMA((3,)),
        ],
        compiler_params=pltpu.CompilerParams(vmem_limit_bytes=20 * 2**20),
    )(*passed)


def solution(mesh):
    in_specs = (
        P(("dp", "dom"), None),
        P(("dp", "dom"), None),
        P(("dp", "dom")),
        P(("dp", "dom")),
        P(("dp", "dom")),
        P(("dp", "dom"), None, None),
        P(),
        P(),
        P(),
        P(),
        P(),
        P(),
        P(),
    )
    out_specs = (P(("dp", "dom"), None), P(("dp", "dom"), None))
    return jax.shard_map(local, mesh=mesh, in_specs=in_specs, out_specs=out_specs, check_vma=False)
```
